512 devices in a mesh: req: 32 (over y_hi, z), cfg: 2 (over core), sp: 8 (over y_lo, x).
Axes of the slice: x: 4, y: 8 (y_hi: 4, y_lo: 2; y = y_hi * 2 + y_lo), z: 8, core: 2. Of those that a mesh axis runs over, the one named last changes fastest.
Arguments:
- vis_qkv: bfloat16 [2, 24576, 3, 16, 128], P('cfg', ('req', 'sp')), parts along dimension 1, may hold values from -26 to 26
- text_kv: bfloat16 [2, 8192, 2, 16, 128], P('cfg', ('req', 'sp')), parts along dimension 1, may hold values from -6 to 6
- text_len: int32 [2, 32], P('cfg', 'req'), parts along dimension 1, may hold values from 1 to 256
- vis_hidden: bfloat16 [2, 24576, 3072], P('cfg', ('req', 'sp')), parts along dimension 1, may hold values from -3 to 3
- out_weight: bfloat16 [2048, 3072], P(None, ('cfg', 'sp')), may hold values from -0.125 to 0.125
- modulation: float32 [2, 96, 3072], P('cfg', 'req'), parts along dimension 1, may hold values from -4 to 4
- final_weight: bfloat16 [3072, 48], replicated, may hold values from -0.0546875 to 0.0546875
- latent: float32 [24576, 48], P(('req', 'sp'), 'cfg'), parts along dimension 0, may hold values from -5 to 5
- timestep: int32 [32], P('req'), parts along dimension 0, may hold values from 0 to 31
Outputs:
- velocity: float32 [24576, 48], P(('req', 'sp'), 'cfg'), parts along dimension 0
- latent_next: float32 [24576, 48], P(('req', 'sp'), 'cfg'), parts along dimension 0
- denoised: float32 [24576, 48], P(('req', 'sp'), 'cfg'), parts along dimension 0
The draws below stay inside these ranges and needn't reach their ends.
There are 32 independent parts, one for each index of `req`. The reference program is written for one: setup_inputs(seed, part) draws one part's arguments, and reference() takes and returns one part's arrays. A program takes and returns all parts, laid end to end along the dimension named above; an argument that names none is the same for every part. Nothing has to cross between parts.
All inputs are finite; a program needn't handle non-finite values.
Results may differ from the reference program's by a relative error of at most 0.0038.
Values may be sent and summed in bfloat16 or wider, within the bound.
No kernel may reach another device: no remote copies, remote signals or barrier semaphores. Data moves between devices by JAX's collectives and lax.ppermute only.
A program may use at most 64 MiB of HBM per device.

```python
import math
import jax
import jax.numpy as jnp
from jax import lax

D = 3072
HEADS = 16
HEAD = 128
PATCH = 48
TXT = 256
STEPS = 64
V = 768


def draw_vis_qkv(key, part):
    key = jax.random.fold_in(key, 11)
    full_shape = (2, V, 3, HEADS, HEAD)
    drawn = 1.5 * jax.random.truncated_normal(key, -4.0, 4.0, full_shape, jnp.float32)
    return drawn.astype(jnp.bfloat16)


def block_scale(key, dims, shards, low, high):
    level = 1.0
    for dim, parts in shards:
        steps = jax.random.uniform(jax.random.fold_in(jax.random.fold_in(key, 6), dim), (parts,), jnp.float32, low / len(shards), high / len(shards))
        level = level * jnp.repeat(jnp.exp(steps), dims[dim] // parts).reshape((-1,) + (1,) * (len(dims) - 1 - dim))
    return level


def scatter_about(own_key, shape, deviation, reach, shards=(), kind=jnp.bfloat16):
    entries = deviation * jax.random.normal(own_key, shape, jnp.float32)
    if shards:
        entries = entries * block_scale(own_key, shape, shards, -0.22, 0.18)
    return jnp.clip(entries, -reach, reach).astype(kind)


def setup_inputs(seed: int = 0, part: int = 0) -> dict:
    key_of = jax.random.split(jax.random.key(seed), 10)
    own_keys = jax.random.split(jax.random.fold_in(key_of[9], part), 10)
    return {
        "vis_qkv": draw_vis_qkv(jax.random.fold_in(jax.random.fold_in(key_of[9], part), 71), part),
        "text_kv": scatter_about(own_keys[1], (2, TXT, 2, HEADS, HEAD), 1.5, 6.0, ((0, 2), (1, 8))),
        "text_len": jax.random.randint(own_keys[2], (2, 1), 1, TXT + 1).astype(jnp.int32),
        "vis_hidden": scatter_about(own_keys[3], (2, V, D), 0.5, 3.0, ((0, 2), (1, 8))),
        "out_weight": scatter_about(key_of[4], (HEADS * HEAD, D), (HEADS * HEAD) ** -0.5, 0.125, ((1, 16),)),
        "modulation": scatter_about(own_keys[5], (2, 3, D), 0.8, 4.0, ((0, 2),), jnp.float32),
        "final_weight": scatter_about(key_of[6], (D, PATCH), (4 * D) ** -0.5, 0.0546875),
        "latent": scatter_about(own_keys[7], (V, PATCH), 1.0, 5.0, ((0, 8), (1, 2)), jnp.float32),
        "timestep": jax.random.randint(own_keys[8], (1,), 0, STEPS // 2).astype(jnp.int32),
    }


def attend_head(query_rows, key_rows, value_rows, key_valid):
    scores = jnp.dot(query_rows, key_rows.T, preferred_element_type=jnp.float32) * (1.0 / math.sqrt(HEAD))
    scores = jnp.where(key_valid[None, :], scores, -1e+30)
    row_peak = lax.optimization_barrier(jnp.max(scores, axis=1, keepdims=True))
    raised = jnp.exp(scores - row_peak)
    weights = (raised / lax.optimization_barrier(jnp.sum(raised, axis=1, keepdims=True))).astype(jnp.bfloat16)
    return jnp.dot(weights, value_rows, preferred_element_type=jnp.float32).astype(jnp.bfloat16)

def branch_pred(qkv_rows, text_rows, length, hidden_rows, mods, out_weight, final_weight):
    key_all = jnp.concatenate([qkv_rows[:, 1], text_rows[:, 0]], axis=0)
    value_all = jnp.concatenate([qkv_rows[:, 2], text_rows[:, 1]], axis=0)
    key_valid = jnp.arange(V + TXT, dtype=jnp.int32) < V + length

    def one_head(items):
        return attend_head(items[0], items[1], items[2], key_valid)
    per_head = lax.map(one_head, (jnp.transpose(qkv_rows[:, 0], (1, 0, 2)), jnp.transpose(key_all, (1, 0, 2)), jnp.transpose(value_all, (1, 0, 2))))
    attended = jnp.transpose(per_head, (1, 0, 2)).reshape(V, HEADS * HEAD)
    projected = jnp.dot(attended, out_weight, preferred_element_type=jnp.float32)
    resid = hidden_rows.astype(jnp.float32) + mods[0] * projected
    center = lax.optimization_barrier(jnp.mean(resid, axis=1, keepdims=True))
    spread = lax.optimization_barrier(jnp.mean((resid - center) * (resid - center), axis=1, keepdims=True))
    normed = (resid - center) * lax.rsqrt(spread + 1e-06)
    modulated = (normed * (1.0 + mods[1]) + mods[2]).astype(jnp.bfloat16)
    return jnp.dot(modulated, final_weight, preferred_element_type=jnp.float32)

def reference(vis_qkv, text_kv, text_len, vis_hidden, out_weight, modulation, final_weight, latent, timestep):
    cond_pred = branch_pred(vis_qkv[0], text_kv[0], text_len[0, 0], vis_hidden[0], modulation[0], out_weight, final_weight)
    uncond_pred = branch_pred(vis_qkv[1], text_kv[1], text_len[1, 0], vis_hidden[1], modulation[1], out_weight, final_weight)
    velocity = uncond_pred + 4.5 * (cond_pred - uncond_pred)
    step_now = timestep[0].astype(jnp.float32)
    remain_now = 1.0 - step_now / STEPS
    remain_next = 1.0 - (step_now + 1.0) / STEPS
    sigma_now = remain_now * remain_now
    sigma_next = remain_next * remain_next
    latent_next = latent + (sigma_next - sigma_now) * velocity
    denoised = latent - sigma_now * velocity
    return (velocity, latent_next, denoised)
```

```python
import functools
import math

import jax
import jax.numpy as jnp
from jax import lax
from jax.experimental import pallas as pl
from jax.experimental.pallas import tpu as pltpu
from jax.sharding import PartitionSpec as P

STEPS = 64
VMEM = 56 << 20
NEG = -1e30
BF = jnp.bfloat16
F32 = jnp.float32
ANY = pl.BlockSpec(memory_space=pl.ANY)
WHOLE = pl.BlockSpec(memory_space=pltpu.VMEM)
SCALARS = pl.BlockSpec(memory_space=pltpu.SMEM)
NT = (((1,), (1,)), ((), ()))


def pack_kernel(vis_ref, txt_ref, o_ref, v_ref, t_ref, out_ref, in_sem, out_sem):
    vis, txt = v_ref.shape[1], t_ref.shape[1]
    loads = [
        pltpu.make_async_copy(vis_ref.at[0, :, j], v_ref.at[j], in_sem.at[j]) for j in range(3)
    ] + [
        pltpu.make_async_copy(txt_ref.at[0, :, j], t_ref.at[j], in_sem.at[3 + j]) for j in range(2)
    ]
    for load in loads:
        load.start()
    stores = []
    at = 0
    for j in range(5):
        loads[j].wait()
        block = v_ref[j] if j < 3 else t_ref[j - 3]
        rows = vis if j < 3 else txt
        out_ref[:, at : at + rows, :] = jnp.swapaxes(block, 0, 1)
        stores.append(
            pltpu.make_async_copy(
                out_ref.at[:, at : at + rows, :], o_ref.at[:, at : at + rows, :], out_sem.at[j]
            )
        )
        stores[-1].start()
        at += rows
    for store in stores:
        store.wait()


def pack(vis_qkv, text_kv):
    _, vis, _, heads, width = vis_qkv.shape
    txt = text_kv.shape[1]
    rows = 3 * vis + 2 * txt
    return pl.pallas_call(
        pack_kernel,
        in_specs=[ANY, ANY],
        out_specs=ANY,
        out_shape=jax.ShapeDtypeStruct((heads, rows, width), BF),
        scratch_shapes=[
            pltpu.VMEM((3, vis, heads, width), BF),
            pltpu.VMEM((2, txt, heads, width), BF),
            pltpu.VMEM((heads, rows, width), BF),
            pltpu.SemaphoreType.DMA((5,)),
            pltpu.SemaphoreType.DMA((5,)),
        ],
        compiler_params=pltpu.CompilerParams(vmem_limit_bytes=VMEM),
        cost_estimate=pl.CostEstimate(
            flops=0, bytes_accessed=4 * heads * rows * width, transcendentals=0
        ),
        name="pack",
    )(vis_qkv, text_kv)


def attend_kernel(len_ref, x_ref, o_ref, k_ref, v_ref):
    src = x_ref.shape[0]
    cols = src // 2
    vis = o_ref.shape[2] // cols
    txt = (x_ref.shape[2] - 3 * vis) // 2
    nv = src * vis
    keys = k_ref.shape[0]
    for i in range(src):
        k_ref[i * vis : (i + 1) * vis, :] = x_ref[i, 0, vis : 2 * vis, :]
        v_ref[i * vis : (i + 1) * vis, :] = x_ref[i, 0, 2 * vis : 3 * vis, :]
        t0 = nv + i * txt
        k_ref[t0 : t0 + txt, :] = x_ref[i, 0, 3 * vis : 3 * vis + txt, :]
        v_ref[t0 : t0 + txt, :] = x_ref[i, 0, 3 * vis + txt : 3 * vis + 2 * txt, :]
    valid = lax.broadcasted_iota(jnp.int32, (1, keys - nv), 1) < len_ref[0]
    scale = math.log2(math.e) / math.sqrt(x_ref.shape[3])
    for i in range(src):
        j = i + 1
        if i % 2:
            continue
        q = jnp.concatenate([x_ref[i, 0, 0:vis, :], x_ref[j, 0, 0:vis, :]], axis=0)
        s = lax.dot_general(q, k_ref[...], NT, preferred_element_type=F32)
        s = jnp.concatenate([s[:, :nv], jnp.where(valid, s[:, nv:], NEG)], axis=1)
        e = jnp.exp2((s - jnp.max(s, axis=1, keepdims=True)) * scale)
        w = (e * (1.0 / jnp.sum(e, axis=1, keepdims=True))).astype(BF)
        o = jnp.dot(w, v_ref[...], preferred_element_type=F32).astype(BF)
        row, at = i // cols, i % cols
        for d in range(row * cols, (row + 1) * cols):
            o_ref[d, 0, at * vis : (at + 2) * vis] = o


def attend(length, x, vis):
    src, heads, rows, width = x.shape
    txt = (rows - 3 * vis) // 2
    keys = src * (vis + txt)
    return pl.pallas_call(
        attend_kernel,
        grid=(heads,),
        in_specs=[SCALARS, pl.BlockSpec((src, 1, rows, width), lambda h: (0, h, 0, 0))],
        out_specs=pl.BlockSpec((src, 1, src // 2 * vis, width), lambda h: (0, h, 0, 0)),
        out_shape=jax.ShapeDtypeStruct((src, heads, src // 2 * vis, width), BF),
        scratch_shapes=[pltpu.VMEM((keys, width), BF), pltpu.VMEM((keys, width), BF)],
        compiler_params=pltpu.CompilerParams(vmem_limit_bytes=VMEM),
        cost_estimate=pl.CostEstimate(
            flops=4 * heads * src * vis * keys * width,
            bytes_accessed=2 * x.size + 4 * heads * src * vis * width,
            transcendentals=heads * src * vis * keys,
        ),
        name="attend",
    )(length, x)


def split2(x):
    hi = x.astype(BF)
    return hi, (x - hi.astype(F32)).astype(BF)


def prepare_kernel(spot_ref, hid_hbm, mod_hbm, fin_hbm, send_hbm, tab_hbm, *refs):
    hid_ref, mod_ref, fin_ref, send_ref, tab_ref, sem = refs
    loads = [
        pltpu.make_async_copy(hid_hbm.at[0], hid_ref, sem.at[0]),
        pltpu.make_async_copy(mod_hbm.at[0], mod_ref, sem.at[1]),
        pltpu.make_async_copy(fin_hbm, fin_ref, sem.at[2]),
    ]
    for load in loads:
        load.start()
    for load in loads:
        load.wait()
    part = send_ref.shape[2] // 4
    patch = fin_ref.shape[0]
    core, row, col = spot_ref[0], spot_ref[1], spot_ref[2]
    windows = []
    for g in range(4):
        c = core if g < 2 else 1 - core
        r = row if g % 2 == 0 else 1 - row
        windows.append(pl.ds(pl.multiple_of((2 * c + r) * (4 * part), 128), 4 * part))
    for g in range(4):
        hid = hid_ref[:, windows[g]]
        for there in range(4):
            at = slice(there * part, (there + 1) * part)
            send_ref[there, :, g * part : (g + 1) * part] = hid[:, at]
    send = pltpu.make_async_copy(send_ref, send_hbm, sem.at[0])
    send.start()
    for me in range(4):

        @pl.when(col == me)
        def _():
            own = slice(me * part, (me + 1) * part)
            total, shift = 0.0, 0.0
            for g in range(4):
                f = fin_ref[:, windows[g]].astype(F32)[:, own]
                scaled = f * (1.0 + mod_ref[1:2, windows[g]][:, own])
                total = total + jnp.sum(scaled, axis=1, keepdims=True)
                moved = f * mod_ref[2:3, windows[g]][:, own]
                shift = shift + jnp.sum(moved, axis=1, keepdims=True)
                tab_ref[g, :patch, :part] = scaled
                gate = mod_ref[0:1, windows[g]][:, own]
                tab_ref[g, patch:, :part] = jnp.broadcast_to(gate, (8, part))
            lane = lax.broadcasted_iota(jnp.int32, (patch, 64), 1)
            tab_ref[0, :patch, part:] = jnp.where(lane == 0, total, shift)

    table = pltpu.make_async_copy(tab_ref, tab_hbm, sem.at[1])
    table.start()
    send.wait()
    table.wait()


def prepare(spot, hidden, modulation, final_t):
    _, vis, width = hidden.shape
    patch = final_t.shape[0]
    part = width // 16
    send, table = (4, vis, 4 * part), (4, patch + 8, part + 64)
    return pl.pallas_call(
        prepare_kernel,
        in_specs=[SCALARS, ANY, ANY, ANY],
        out_specs=[ANY, ANY],
        out_shape=[jax.ShapeDtypeStruct(send, BF), jax.ShapeDtypeStruct(table, F32)],
        scratch_shapes=[
            pltpu.VMEM((vis, width), BF),
            pltpu.VMEM(modulation.shape[1:], F32),
            pltpu.VMEM(final_t.shape, BF),
            pltpu.VMEM(send, BF),
            pltpu.VMEM(table, F32),
            pltpu.SemaphoreType.DMA((3,)),
        ],
        compiler_params=pltpu.CompilerParams(vmem_limit_bytes=VMEM),
        name="prepare",
    )(spot, hidden, modulation, final_t)


def project_kernel(a_ref, *refs):
    w_hbm, (got_hbm, tab_hbm, o_ref) = refs[:4], refs[4:7]
    w_ref, got_ref, tab_ref, lhs_ref, r_ref, sem = refs[7:]
    chunks, tokens, depth = a_ref.shape
    vis = tokens // 4
    part = r_ref.shape[2]
    patch = tab_ref.shape[1] - 8
    loads = [pltpu.make_async_copy(w_hbm[g], w_ref.at[g], sem.at[g]) for g in range(4)]
    loads.append(pltpu.make_async_copy(got_hbm, got_ref, sem.at[4]))
    loads.append(pltpu.make_async_copy(tab_hbm, tab_ref, sem.at[5]))
    for i in (0, 4, 5, 1, 2, 3):
        loads[i].start()
    for i in range(chunks):
        lhs_ref[:, i * depth : (i + 1) * depth] = a_ref[i]
    total = 0.0
    for g in range(4):
        loads[g].wait()
        p = lax.dot_general(lhs_ref[...], w_ref[g], NT, preferred_element_type=F32)
        if g == 0:
            loads[4].wait()
            loads[5].wait()
        h = jnp.concatenate([got_ref[k, :, g * part : (g + 1) * part] for k in range(4)], axis=0)
        r = h.astype(F32) + tab_ref[g, patch : patch + 1, :part] * p
        r_ref[g] = r
        total = total + jnp.sum(r, axis=1, keepdims=True)
    mean = total * (1.0 / (4 * part))
    spread = 0.0
    pred = jnp.zeros((patch, tokens), F32)
    for g in range(4):
        d = r_ref[g] - mean
        spread = spread + jnp.sum(d * d, axis=1, keepdims=True)
        hi, lo = split2(d)
        w_hi, w_lo = split2(tab_ref[g, :patch, :part])
        pred = pred + lax.dot_general(w_hi, hi, NT, preferred_element_type=F32)
        pred = pred + lax.dot_general(w_hi, lo, NT, preferred_element_type=F32)
        pred = pred + lax.dot_general(w_lo, hi, NT, preferred_element_type=F32)
    lane = lax.broadcasted_iota(jnp.int32, (tokens, 128), 1)
    stats = jnp.transpose(jnp.where(lane == 0, mean, spread))[:8]
    sums = tab_ref[0, :patch, part : part + 32]
    half = patch // 2
    for c in range(2):
        for k in range(4):
            at = slice(k * vis, (k + 1) * vis)
            rows = slice(c * half, (c + 1) * half)
            o_ref[c * 4 + k, :half] = jnp.concatenate([pred[rows, at], sums[rows]], axis=1)
            o_ref[c * 4 + k, half:] = jnp.concatenate([stats[:, at], stats[:, :32]], axis=1)


def project(att, blocks, got, table):
    chunks, tokens, width = att.shape
    cols, depth = blocks[0].shape
    patch = table.shape[1] - 8
    return pl.pallas_call(
        project_kernel,
        in_specs=[WHOLE] + [ANY] * 6,
        out_specs=WHOLE,
        out_shape=jax.ShapeDtypeStruct((8, patch // 2 + 8, 128), F32),
        scratch_shapes=[
            pltpu.VMEM((4, cols, depth), BF),
            pltpu.VMEM(got.shape, BF),
            pltpu.VMEM(table.shape, F32),
            pltpu.VMEM((tokens, depth), BF),
            pltpu.VMEM((4, tokens, cols), F32),
            pltpu.SemaphoreType.DMA((6,)),
        ],
        compiler_params=pltpu.CompilerParams(vmem_limit_bytes=VMEM),
        cost_estimate=pl.CostEstimate(
            flops=8 * cols * depth * tokens,
            bytes_accessed=8 * cols * depth,
            transcendentals=0,
        ),
        name="project",
    )(att, *blocks, got, table)


def update_kernel(step_ref, x_ref, lat_ref, vel_ref, next_ref, den_ref, *, count):
    half, vis = lat_ref.shape
    preds = []
    for b in range(2):
        parts = [x_ref[b * 4 + k] for k in range(4)]
        means = [t[half : half + 1, :vis] for t in parts]
        mean = 0.25 * (means[0] + means[1] + means[2] + means[3])
        spread, linear, shift = 0.0, 0.0, 0.0
        for k in range(4):
            off = means[k] - mean
            spread = spread + parts[k][half + 1 : half + 2, :vis] + (0.25 * count) * (off * off)
            linear = linear + parts[k][:half, :vis] + parts[k][:half, vis : vis + 1] * off
            shift = shift + parts[k][:half, vis + 1 : vis + 2]
        preds.append(linear * lax.rsqrt(spread * (1.0 / count) + 1e-06) + shift)
    cond, uncond = preds
    velocity = uncond + 4.5 * (cond - uncond)
    step_now = step_ref[0].astype(F32)
    remain_now = 1.0 - step_now * (1.0 / STEPS)
    remain_next = 1.0 - (step_now + 1.0) * (1.0 / STEPS)
    sigma_now = remain_now * remain_now
    sigma_next = remain_next * remain_next
    latent = lat_ref[...]
    vel_ref[...] = velocity
    next_ref[...] = latent + (sigma_next - sigma_now) * velocity
    den_ref[...] = latent - sigma_now * velocity


def update(timestep, parts, latent, count):
    return pl.pallas_call(
        functools.partial(update_kernel, count=count),
        in_specs=[SCALARS, WHOLE, WHOLE],
        out_specs=[WHOLE] * 3,
        out_shape=[jax.ShapeDtypeStruct(latent.shape, F32)] * 3,
        name="update",
    )(timestep, parts, latent)


def across_outer(reqs):
    deep = 8
    if reqs % deep:
        return None
    high = reqs // deep
    pairs = []
    for r in range(reqs):
        for s in range(8):
            y = 2 * (r // deep) + s // 4
            near = (y + 1 if y % 2 else y - 1) % (2 * high)
            pairs.append((r * 8 + s, (near // 2 * deep + r % deep) * 8 + near % 2 * 4 + s % 4))
    return pairs


def shards(
    vis_qkv, text_kv, text_len, vis_hidden, out_weight, modulation, final_weight, latent, timestep
):
    vis, txt = vis_qkv.shape[1], text_kv.shape[1]
    spot = jnp.stack([lax.axis_index(a) for a in ("cfg", "row", "col")])
    cores = [(0, 1), (1, 0)]
    outer = across_outer(lax.axis_size("req"))

    own = out_weight.T

    def across(block):
        if outer is None:
            return lax.ppermute(block, "row", cores)
        return lax.ppermute(block, ("req", "row", "col"), outer)

    far = across(own)
    own_other = lax.ppermute(own, "cfg", cores)
    packed, spot = lax.optimization_barrier((pack(vis_qkv, text_kv), spot))
    heads = lax.all_to_all(
        packed, ("row", "col"), split_axis=0, concat_axis=0, tiled=True
    ).reshape(8, 2, 3 * vis + 2 * txt, 128)
    send, table = prepare(spot, vis_hidden, modulation, final_weight.T)
    heads, own_other, send = lax.optimization_barrier((heads, own_other, send))
    got = lax.all_to_all(send, "col", split_axis=0, concat_axis=0, tiled=True)
    attended = attend(text_len[0], heads, vis)
    attended, far, got = lax.optimization_barrier((attended, far, got))
    far_other = lax.ppermute(far, "cfg", cores)
    att = lax.all_to_all(
        attended, ("row", "col"), split_axis=0, concat_axis=0, tiled=True
    ).reshape(16, 4 * vis, 128)
    parts = project(att, [own, far, own_other, far_other], got, table)
    parts = lax.all_to_all(parts, ("cfg", "col"), split_axis=0, concat_axis=0, tiled=True)
    outs = update(timestep, parts, latent.T, vis_hidden.shape[2])
    return tuple(o.T for o in outs)


def solution(mesh):
    req, cfg, sp = mesh.devices.shape
    fine = jax.sharding.Mesh(
        mesh.devices.reshape(req, cfg, 2, sp // 2), ("req", "cfg", "row", "col")
    )
    tokens = ("req", "row", "col")
    out = P(tokens, "cfg")
    return jax.shard_map(
        shards,
        mesh=fine,
        in_specs=(
            P("cfg", tokens, None, None, None),
            P("cfg", tokens, None, None, None),
            P("cfg", "req"),
            P("cfg", tokens, None),
            P(None, ("cfg", "row", "col")),
            P("cfg", "req", None),
            P(),
            out,
            P("req"),
        ),
        out_specs=(out, out, out),
        check_vma=False,
    )
```

```python
import functools
import math

import jax
import jax.numpy as jnp
from jax import lax
from jax.experimental import pallas as pl
from jax.experimental.pallas import tpu as pltpu
from jax.sharding import PartitionSpec as P

STEPS = 64
SMALL = 16 << 20
LARGE = 56 << 20
MOST = 51 << 20
NEG = -1e30
BF = jnp.bfloat16
F32 = jnp.float32
ANY = pl.BlockSpec(memory_space=pltpu.HBM)
WHOLE = pl.BlockSpec(memory_space=pltpu.VMEM)
SCALARS = pl.BlockSpec(memory_space=pltpu.SMEM)
NT = (((1,), (1,)), ((), ()))


def windows(core, row, width):
    starts = []
    for c in (core, 1 - core):
        for r in (row, 1 - row):
            starts.append(pl.ds(pl.multiple_of((2 * c + r) * width, 128), width))
    return starts


def pack_kernel(vis_ref, txt_ref, hid_hbm, o_ref, *refs):
    sends, (v_ref, t_ref, hid_ref, out_ref, send_ref, in_sem, out_sem) = refs[:4], refs[4:]
    vis, txt = v_ref.shape[1], t_ref.shape[1]
    loads = [
        pltpu.make_async_copy(vis_ref.at[0, :, j], v_ref.at[j], in_sem.at[j]) for j in range(3)
    ] + [
        pltpu.make_async_copy(txt_ref.at[0, :, j], t_ref.at[j], in_sem.at[3 + j]) for j in range(2)
    ]
    loads.append(pltpu.make_async_copy(hid_hbm.at[0], hid_ref, in_sem.at[5]))
    for load in loads:
        load.start()
    stores = []
    at = 0
    for j in range(5):
        loads[j].wait()
        block = v_ref[j] if j < 3 else t_ref[j - 3]
        rows = vis if j < 3 else txt
        out_ref[:, at : at + rows, :] = jnp.swapaxes(block, 0, 1)
        stores.append(
            pltpu.make_async_copy(
                out_ref.at[:, at : at + rows, :], o_ref.at[:, at : at + rows, :], out_sem.at[j]
            )
        )
        stores[-1].start()
        at += rows
    loads[5].wait()
    core, row, col = (lax.axis_index(a) for a in ("cfg", "row", "col"))
    part = send_ref.shape[2] // 4
    for me in range(4):

        @pl.when(col == me)
        def _():
            for g, window in enumerate(windows(core, row, 4 * part)):
                hid = hid_ref[:, window]
                for d in range(4):
                    there = me ^ d
                    at = slice(there * part, (there + 1) * part)
                    send_ref[d, :, g * part : (g + 1) * part] = hid[:, at]

    for d in range(4):
        stores.append(pltpu.make_async_copy(send_ref.at[d], sends[d], out_sem.at[5 + d]))
        stores[-1].start()
    for store in stores:
        store.wait()


def pack(vis_qkv, text_kv, hidden):
    _, vis, _, heads, width = vis_qkv.shape
    txt = text_kv.shape[1]
    rows = 3 * vis + 2 * txt
    quarter = hidden.shape[2] // 4
    return pl.pallas_call(
        pack_kernel,
        in_specs=[ANY] * 3,
        out_specs=[ANY] * 5,
        out_shape=[jax.ShapeDtypeStruct((heads, rows, width), BF)]
        + [jax.ShapeDtypeStruct((vis, quarter), BF)] * 4,
        scratch_shapes=[
            pltpu.VMEM((3, vis, heads, width), BF),
            pltpu.VMEM((2, txt, heads, width), BF),
            pltpu.VMEM(hidden.shape[1:], BF),
            pltpu.VMEM((heads, rows, width), BF),
            pltpu.VMEM((4, vis, quarter), BF),
            pltpu.SemaphoreType.DMA((6,)),
            pltpu.SemaphoreType.DMA((9,)),
        ],
        compiler_params=pltpu.CompilerParams(vmem_limit_bytes=LARGE),
        cost_estimate=pl.CostEstimate(
            flops=0, bytes_accessed=4 * heads * rows * width, transcendentals=0
        ),
        name="pack",
    )(vis_qkv, text_kv, hidden)


def attend_kernel(len_ref, x_ref, o_hbm, k_ref, v_ref, o_ref, sem):
    src, heads, rows, width = x_ref.shape
    cols = src // 2
    vis = o_ref.shape[2] // 2
    txt = (rows - 3 * vis) // 2
    nv = src * vis
    keys = k_ref.shape[1]
    valid = lax.broadcasted_iota(jnp.int32, (1, keys - nv), 1) < len_ref[0]
    scale = math.log2(math.e) / math.sqrt(width)
    ones = jnp.ones((keys, width), BF)
    stores = []
    for h in range(heads):
        for i in range(src):
            at, t0 = slice(i * vis, (i + 1) * vis), nv + i * txt
            k_ref[h, at, :] = x_ref[i, h, vis : 2 * vis, :]
            v_ref[h, at, :width] = x_ref[i, h, 2 * vis : 3 * vis, :]
            k_ref[h, t0 : t0 + txt, :] = x_ref[i, h, 3 * vis : 3 * vis + txt, :]
            v_ref[h, t0 : t0 + txt, :width] = x_ref[i, h, 3 * vis + txt : 3 * vis + 2 * txt, :]
        v_ref[h, :, width:] = ones
        for i in range(0, src, 2):
            q = jnp.concatenate([x_ref[i, h, 0:vis, :], x_ref[i + 1, h, 0:vis, :]], axis=0)
            s = lax.dot_general(q, k_ref[h], NT, preferred_element_type=F32)
            s = jnp.concatenate([s[:, :nv], jnp.where(valid, s[:, nv:], NEG)], axis=1)
            e = jnp.exp2((s - jnp.max(s, axis=1, keepdims=True)) * scale)
            o = jnp.dot(e.astype(BF), v_ref[h], preferred_element_type=F32)
            n = h * src + i
            o_ref[h, i // 2] = (o[:, :width] / o[:, width:]).astype(BF)
            row, at = i // cols, (i % cols) * vis
            for d in range(row * cols, (row + 1) * cols):
                stores.append(
                    pltpu.make_async_copy(
                        o_ref.at[h, i // 2], o_hbm.at[d, h, pl.ds(at, 2 * vis)], sem.at[n + d % 2]
                    )
                )
                stores[-1].start()
    for store in stores:
        store.wait()


def attend(length, x, vis):
    src, heads, rows, width = x.shape
    txt = (rows - 3 * vis) // 2
    keys = src * (vis + txt)
    return pl.pallas_call(
        attend_kernel,
        in_specs=[SCALARS, WHOLE],
        out_specs=ANY,
        out_shape=jax.ShapeDtypeStruct((src, heads, src // 2 * vis, width), BF),
        scratch_shapes=[
            pltpu.VMEM((heads, keys, width), BF),
            pltpu.VMEM((heads, keys, 2 * width), BF),
            pltpu.VMEM((heads, src // 2, 2 * vis, width), BF),
            pltpu.SemaphoreType.DMA((heads * src,)),
        ],
        compiler_params=pltpu.CompilerParams(vmem_limit_bytes=SMALL),
        cost_estimate=pl.CostEstimate(
            flops=4 * heads * src * vis * keys * width,
            bytes_accessed=2 * x.size + 4 * heads * src * vis * width,
            transcendentals=heads * src * vis * keys,
        ),
        name="attend",
    )(length, x)


def split2(x):
    hi = x.astype(BF)
    return hi, (x - hi.astype(F32)).astype(BF)


def split3(x):
    a = x.astype(BF)
    rest = x - a.astype(F32)
    b = rest.astype(BF)
    return a, b, (rest - b.astype(F32)).astype(BF)


def places(cols, vis, patch):
    rows = 2 * patch + 16
    blocks = [(slice(g * cols, (g + 1) * cols), slice(0, None)) for g in range(4)]
    hidden, tables = [], []
    for k in range(4):
        at, across = 4 * cols + (k // 2) * vis, (k % 2) * 4 * cols
        hidden.append((slice(at, at + vis), slice(across, across + 4 * cols)))
        at, across = 4 * cols + (k // 2) * rows, 8 * cols + (k % 2) * (cols + 64)
        tables.append((slice(at, at + rows), slice(across, across + cols + 64)))
    return blocks, hidden, tables


def stage_kernel(mod_hbm, fin_hbm, *refs):
    w_hbm, got_hbm, out_hbm = refs[:4], refs[4:8], refs[8]
    mod_ref, fin_ref, all_ref, sem = refs[9:]
    core, row, col = (lax.axis_index(a) for a in ("cfg", "row", "col"))
    part, vis = w_hbm[0].shape[0], got_hbm[0].shape[0]
    patch = fin_ref.shape[0]
    blocks, hidden, tables = places(part, vis, patch)
    loads = [
        pltpu.make_async_copy(mod_hbm.at[0], mod_ref, sem.at[0]),
        pltpu.make_async_copy(fin_hbm, fin_ref, sem.at[1]),
    ]
    moves = [pltpu.make_async_copy(w_hbm[g], all_ref.at[blocks[g]], sem.at[2 + g]) for g in range(4)]
    for load in loads + moves:
        load.start()
    for load in loads:
        load.wait()
    for me in range(4):

        @pl.when(col == me)
        def _():
            copies = [
                pltpu.make_async_copy(got_hbm[d], all_ref.at[hidden[me ^ d]], sem.at[6 + d])
                for d in range(4)
            ]
            for copy in copies:
                copy.start()
            own = slice(me * part, (me + 1) * part)
            total, shift = 0.0, 0.0
            for g, window in enumerate(windows(core, row, 4 * part)):
                f = fin_ref[:, window].astype(F32)[:, own]
                scaled = f * (1.0 + mod_ref[1:2, window][:, own])
                total = total + jnp.sum(scaled, axis=1, keepdims=True)
                moved = f * mod_ref[2:3, window][:, own]
                shift = shift + jnp.sum(moved, axis=1, keepdims=True)
                hi, lo = split2(scaled)
                gate = split3(jnp.broadcast_to(mod_ref[0:1, window][:, own], (16, part)))
                line = lax.broadcasted_iota(jnp.int32, (16, part), 0)
                gate = jnp.where(line == 0, gate[0], jnp.where(line == 1, gate[1], gate[2]))
                both = jnp.concatenate([hi, lo, gate], axis=0)
                extra = jnp.zeros((both.shape[0], 64), BF)
                if g == 3:
                    lane = lax.broadcasted_iota(jnp.int32, (patch, 64), 1)
                    pieces = split3(jnp.where(lane % 2 == 0, total, shift))
                    pieces = jnp.where(
                        lane < 2, pieces[0], jnp.where(lane < 4, pieces[1], pieces[2])
                    )
                    extra = jnp.concatenate([pieces, extra[patch:]], axis=0)
                all_ref[tables[g]] = jnp.concatenate([both, extra], axis=1)
            for copy in copies:
                copy.wait()

    for move in moves:
        move.wait()
    store = pltpu.make_async_copy(all_ref, out_hbm, sem.at[0])
    store.start()
    store.wait()


def stage(modulation, final_t, blocks, got):
    patch, width = final_t.shape
    cols, depth = blocks[0].shape
    rows = 4 * cols + 2 * max(got[0].shape[0], 2 * patch + 16)
    return pl.pallas_call(
        stage_kernel,
        in_specs=[ANY] * 10,
        out_specs=ANY,
        out_shape=jax.ShapeDtypeStruct((rows, depth), BF),
        scratch_shapes=[
            pltpu.VMEM(modulation.shape[1:], F32),
            pltpu.VMEM(final_t.shape, BF),
            pltpu.VMEM((rows, depth), BF),
            pltpu.SemaphoreType.DMA((10,)),
        ],
        compiler_params=pltpu.CompilerParams(vmem_limit_bytes=LARGE),
        cost_estimate=pl.CostEstimate(flops=2 * 10**10, bytes_accessed=0, transcendentals=0),
        name="stage",
    )(modulation, final_t, *blocks, *got)


def project_kernel(a_ref, all_hbm, o_ref, w_ref, hid_ref, tab_ref, lhs_ref, r_ref, sem):
    chunks, tokens, depth = a_ref.shape
    vis = tokens // 4
    part = r_ref.shape[2]
    patch = 2 * o_ref.shape[1] - 16
    blocks, hidden, tables = places(part, vis, patch)
    loads, rest = [], []
    for k in range(4):
        w = pltpu.make_async_copy(all_hbm.at[blocks[k]], w_ref.at[k], sem.at[k])
        h = pltpu.make_async_copy(all_hbm.at[hidden[k]], hid_ref.at[k], sem.at[4 + k])
        t = pltpu.make_async_copy(all_hbm.at[tables[k]], tab_ref.at[k], sem.at[8 + k])
        loads.append(w)
        rest += [h, t]
    for load in loads + rest:
        load.start()
    for i in range(chunks):
        lhs_ref[:, i * depth : (i + 1) * depth] = a_ref[i]
    for g in range(4):
        loads[g].wait()
        r_ref[g] = lax.dot_general(lhs_ref[...], w_ref[g], NT, preferred_element_type=F32)
    for load in rest:
        load.wait()
    total = 0.0
    for g in range(4):
        h = jnp.concatenate([hid_ref[k, :, g * part : (g + 1) * part] for k in range(4)], axis=0)
        gate = tab_ref[g, 2 * patch :, :part].astype(F32)
        r = h.astype(F32) + (gate[0:1] + gate[1:2] + gate[2:3]) * r_ref[g]
        r_ref[g] = r
        total = total + r
    mean = jnp.sum(total, axis=1, keepdims=True) * (1.0 / (4 * part))
    spread = 0.0
    pred = jnp.zeros((patch, tokens), F32)
    for g in range(4):
        d = r_ref[g] - mean
        spread = spread + d * d
        hi, lo = split2(d)
        w_hi, w_lo = tab_ref[g, :patch, :part], tab_ref[g, patch : 2 * patch, :part]
        pred = pred + lax.dot_general(w_hi, hi, NT, preferred_element_type=F32)
        pred = pred + lax.dot_general(w_hi, lo, NT, preferred_element_type=F32)
        pred = pred + lax.dot_general(w_lo, hi, NT, preferred_element_type=F32)
    spread = jnp.sum(spread, axis=1, keepdims=True)
    lane = lax.broadcasted_iota(jnp.int32, (tokens, 128), 1)
    stats = jnp.transpose(jnp.where(lane == 0, mean, spread))[:8]
    sums = tab_ref[3, :patch, part:].astype(F32)
    sums = (sums[:, :32] + sums[:, 2:34]) + sums[:, 4:36]
    half = patch // 2
    for c in range(2):
        for k in range(4):
            at = slice(k * vis, (k + 1) * vis)
            rows = slice(c * half, (c + 1) * half)
            o_ref[c * 4 + k, :half] = jnp.concatenate([pred[rows, at], sums[rows]], axis=1)
            o_ref[c * 4 + k, half:] = jnp.concatenate([stats[:, at], stats[:, :32]], axis=1)


def project(att, staged, patch):
    chunks, tokens, width = att.shape
    depth = chunks * width
    vis = tokens // 4
    cols = depth * 3 // 32
    return pl.pallas_call(
        project_kernel,
        in_specs=[WHOLE, ANY],
        out_specs=WHOLE,
        out_shape=jax.ShapeDtypeStruct((8, patch // 2 + 8, 128), F32),
        scratch_shapes=[
            pltpu.VMEM((4, cols, depth), BF),
            pltpu.VMEM((4, vis, 4 * cols), BF),
            pltpu.VMEM((4, 2 * patch + 16, cols + 64), BF),
            pltpu.VMEM((tokens, depth), BF),
            pltpu.VMEM((4, tokens, cols), F32),
            pltpu.SemaphoreType.DMA((12,)),
        ],
        compiler_params=pltpu.CompilerParams(vmem_limit_bytes=MOST),
        cost_estimate=pl.CostEstimate(
            flops=8 * cols * depth * tokens,
            bytes_accessed=8 * cols * depth,
            transcendentals=0,
        ),
        name="project",
    )(att, staged)


def update_kernel(step_ref, x_ref, lat_ref, vel_ref, next_ref, den_ref, *, count):
    half, vis = lat_ref.shape
    preds = []
    for b in range(2):
        parts = [x_ref[b * 4 + k] for k in range(4)]
        means = [t[half : half + 1, :vis] for t in parts]
        mean = 0.25 * (means[0] + means[1] + means[2] + means[3])
        spread, linear, shift = 0.0, 0.0, 0.0
        for k in range(4):
            off = means[k] - mean
            spread = spread + parts[k][half + 1 : half + 2, :vis] + (0.25 * count) * (off * off)
            linear = linear + parts[k][:half, :vis] + parts[k][:half, vis : vis + 1] * off
            shift = shift + parts[k][:half, vis + 1 : vis + 2]
        preds.append(linear * lax.rsqrt(spread * (1.0 / count) + 1e-06) + shift)
    cond, uncond = preds
    velocity = uncond + 4.5 * (cond - uncond)
    step_now = step_ref[0].astype(F32)
    remain_now = 1.0 - step_now * (1.0 / STEPS)
    remain_next = 1.0 - (step_now + 1.0) * (1.0 / STEPS)
    sigma_now = remain_now * remain_now
    sigma_next = remain_next * remain_next
    latent = lat_ref[...]
    vel_ref[...] = velocity
    next_ref[...] = latent + (sigma_next - sigma_now) * velocity
    den_ref[...] = latent - sigma_now * velocity


def update(timestep, parts, latent, count):
    return pl.pallas_call(
        functools.partial(update_kernel, count=count),
        in_specs=[SCALARS, WHOLE, WHOLE],
        out_specs=[WHOLE] * 3,
        out_shape=[jax.ShapeDtypeStruct(latent.shape, F32)] * 3,
        compiler_params=pltpu.CompilerParams(vmem_limit_bytes=2 << 20),
        name="update",
    )(timestep, parts, latent)


def across_outer(reqs):
    deep = 8
    if reqs % deep:
        return None
    high = reqs // deep
    pairs = []
    for r in range(reqs):
        for s in range(8):
            y = 2 * (r // deep) + s // 4
            near = (y + 1 if y % 2 else y - 1) % (2 * high)
            pairs.append((r * 8 + s, (near // 2 * deep + r % deep) * 8 + near % 2 * 4 + s % 4))
    return pairs


def shards(
    vis_qkv, text_kv, text_len, vis_hidden, out_weight, modulation, final_weight, latent, timestep
):
    vis, txt = vis_qkv.shape[1], text_kv.shape[1]
    cores = [(0, 1), (1, 0)]
    outer = across_outer(lax.axis_size("req"))

    own = out_weight.T

    def across(block):
        if outer is None:
            return lax.ppermute(block, "row", cores)
        return lax.ppermute(block, ("req", "row", "col"), outer)

    far = across(own)
    packed, mine, *sends = pack(vis_qkv, text_kv, vis_hidden)
    heads = lax.all_to_all(
        packed, ("row", "col"), split_axis=0, concat_axis=0, tiled=True
    ).reshape(8, 2, 3 * vis + 2 * txt, 128)
    got = [mine] + [
        lax.ppermute(block, "col", [(c, c ^ d) for c in range(4)])
        for d, block in zip((1, 2, 3), sends)
    ]
    attended = attend(text_len[0], heads, vis)
    far, modulation, *got = lax.optimization_barrier((far, modulation, *got))
    own_other, far_other = (lax.ppermute(b, "cfg", cores) for b in (own, far))
    staged = stage(modulation, final_weight.T, [own, far, own_other, far_other], got)
    att = lax.all_to_all(
        attended, ("row", "col"), split_axis=0, concat_axis=0, tiled=True
    ).reshape(16, 4 * vis, 128)
    parts = project(att, staged, final_weight.shape[1])
    parts = lax.all_to_all(parts, ("cfg", "col"), split_axis=0, concat_axis=0, tiled=True)
    outs = update(timestep, parts, latent.T, vis_hidden.shape[2])
    return tuple(o.T for o in outs)


def solution(mesh):
    req, cfg, sp = mesh.devices.shape
    fine = jax.sharding.Mesh(
        mesh.devices.reshape(req, cfg, 2, sp // 2), ("req", "cfg", "row", "col")
    )
    tokens = ("req", "row", "col")
    out = P(tokens, "cfg")
    return jax.shard_map(
        shards,
        mesh=fine,
        in_specs=(
            P("cfg", tokens, None, None, None),
            P("cfg", tokens, None, None, None),
            P("cfg", "req"),
            P("cfg", tokens, None),
            P(None, ("cfg", "row", "col")),
            P("cfg", "req", None),
            P(),
            out,
            P("req"),
        ),
        out_specs=(out, out, out),
        check_vma=False,
    )
```

```python
import functools
import math

import jax
import jax.numpy as jnp
from jax import lax
from jax.experimental import pallas as pl
from jax.experimental.pallas import tpu as pltpu
from jax.sharding import PartitionSpec as P

STEPS = 64
SMALL = 16 << 20
LARGE = 56 << 20
MOST = 51 << 20
STAGE = 10 << 20
NEG = -1e30
BF = jnp.bfloat16
F32 = jnp.float32
ANY = pl.BlockSpec(memory_space=pltpu.HBM)
WHOLE = pl.BlockSpec(memory_space=pltpu.VMEM)
SCALARS = pl.BlockSpec(memory_space=pltpu.SMEM)
NT = (((1,), (1,)), ((), ()))


def windows(core, row, width):
    starts = []
    for c in (core, 1 - core):
        for r in (row, 1 - row):
            starts.append(pl.ds(pl.multiple_of((2 * c + r) * width, 128), width))
    return starts


def pack_kernel(vis_ref, txt_ref, o_ref, v_ref, t_ref, out_ref, in_sem, out_sem):
    vis, txt = v_ref.shape[1], t_ref.shape[1]
    loads = [
        pltpu.make_async_copy(vis_ref.at[0, :, j], v_ref.at[j], in_sem.at[j]) for j in range(3)
    ] + [
        pltpu.make_async_copy(txt_ref.at[0, :, j], t_ref.at[j], in_sem.at[3 + j]) for j in range(2)
    ]
    for load in loads:
        load.start()
    stores = []
    at = 0
    for j in range(5):
        loads[j].wait()
        block = v_ref[j] if j < 3 else t_ref[j - 3]
        rows = vis if j < 3 else txt
        out_ref[:, at : at + rows, :] = jnp.swapaxes(block, 0, 1)
        stores.append(
            pltpu.make_async_copy(
                out_ref.at[:, at : at + rows, :], o_ref.at[:, at : at + rows, :], out_sem.at[j]
            )
        )
        stores[-1].start()
        at += rows
    for store in stores:
        store.wait()


def pack(vis_qkv, text_kv):
    _, vis, _, heads, width = vis_qkv.shape
    txt = text_kv.shape[1]
    rows = 3 * vis + 2 * txt
    return pl.pallas_call(
        pack_kernel,
        in_specs=[ANY, ANY],
        out_specs=ANY,
        out_shape=jax.ShapeDtypeStruct((heads, rows, width), BF),
        scratch_shapes=[
            pltpu.VMEM((3, vis, heads, width), BF),
            pltpu.VMEM((2, txt, heads, width), BF),
            pltpu.VMEM((heads, rows, width), BF),
            pltpu.SemaphoreType.DMA((5,)),
            pltpu.SemaphoreType.DMA((5,)),
        ],
        compiler_params=pltpu.CompilerParams(vmem_limit_bytes=LARGE),
        cost_estimate=pl.CostEstimate(
            flops=0, bytes_accessed=4 * heads * rows * width, transcendentals=0
        ),
        name="pack",
    )(vis_qkv, text_kv)


def share_kernel(hid_hbm, *refs):
    sends, (hid_ref, sem) = refs[:4], refs[4:]
    load = pltpu.make_async_copy(hid_hbm.at[0], hid_ref, sem)
    load.start()
    core, row, col = (lax.axis_index(a) for a in ("cfg", "row", "col"))
    part = sends[0].shape[1] // 4
    load.wait()
    for me in range(4):

        @pl.when(col == me)
        def _():
            for g, window in enumerate(windows(core, row, 4 * part)):
                hid = hid_ref[:, window]
                for d in range(4):
                    there = me ^ d
                    at = slice(there * part, (there + 1) * part)
                    sends[d][:, g * part : (g + 1) * part] = hid[:, at]


def share(hidden):
    _, vis, width = hidden.shape
    return pl.pallas_call(
        share_kernel,
        in_specs=[ANY],
        out_specs=[WHOLE] * 4,
        out_shape=[jax.ShapeDtypeStruct((vis, width // 4), BF)] * 4,
        scratch_shapes=[pltpu.VMEM((vis, width), BF), pltpu.SemaphoreType.DMA],
        compiler_params=pltpu.CompilerParams(vmem_limit_bytes=LARGE),
        name="share",
    )(hidden)


def attend_kernel(len_ref, x_ref, o_hbm, k_ref, v_ref, o_ref, sem):
    src, heads, rows, width = x_ref.shape
    cols = src // 2
    vis = o_ref.shape[2] // 2
    txt = (rows - 3 * vis) // 2
    nv = src * vis
    keys = k_ref.shape[1]
    valid = lax.broadcasted_iota(jnp.int32, (1, keys - nv), 1) < len_ref[0]
    scale = math.log2(math.e) / math.sqrt(width)
    ones = jnp.ones((keys, width), BF)
    stores = []
    for h in range(heads):
        for i in range(src):
            at, t0 = slice(i * vis, (i + 1) * vis), nv + i * txt
            k_ref[h, at, :] = x_ref[i, h, vis : 2 * vis, :]
            v_ref[h, at, :width] = x_ref[i, h, 2 * vis : 3 * vis, :]
            k_ref[h, t0 : t0 + txt, :] = x_ref[i, h, 3 * vis : 3 * vis + txt, :]
            v_ref[h, t0 : t0 + txt, :width] = x_ref[i, h, 3 * vis + txt : 3 * vis + 2 * txt, :]
        v_ref[h, :, width:] = ones
        for i in range(0, src, 2):
            q = jnp.concatenate([x_ref[i, h, 0:vis, :], x_ref[i + 1, h, 0:vis, :]], axis=0)
            s = lax.dot_general(q, k_ref[h], NT, preferred_element_type=F32)
            s = jnp.concatenate([s[:, :nv], jnp.where(valid, s[:, nv:], NEG)], axis=1)
            e = jnp.exp2((s - jnp.max(s, axis=1, keepdims=True)) * scale)
            o = jnp.dot(e.astype(BF), v_ref[h], preferred_element_type=F32)
            n = h * src + i
            o_ref[h, i // 2] = (o[:, :width] / o[:, width:]).astype(BF)
            row, at = i // cols, (i % cols) * vis
            for d in range(row * cols, (row + 1) * cols):
                stores.append(
                    pltpu.make_async_copy(
                        o_ref.at[h, i // 2], o_hbm.at[d, h, pl.ds(at, 2 * vis)], sem.at[n + d % 2]
                    )
                )
                stores[-1].start()
    for store in stores:
        store.wait()


def attend(length, x, vis):
    src, heads, rows, width = x.shape
    txt = (rows - 3 * vis) // 2
    keys = src * (vis + txt)
    return pl.pallas_call(
        attend_kernel,
        in_specs=[SCALARS, WHOLE],
        out_specs=ANY,
        out_shape=jax.ShapeDtypeStruct((src, heads, src // 2 * vis, width), BF),
        scratch_shapes=[
            pltpu.VMEM((heads, keys, width), BF),
            pltpu.VMEM((heads, keys, 2 * width), BF),
            pltpu.VMEM((heads, src // 2, 2 * vis, width), BF),
            pltpu.SemaphoreType.DMA((heads * src,)),
        ],
        compiler_params=pltpu.CompilerParams(vmem_limit_bytes=SMALL),
        cost_estimate=pl.CostEstimate(
            flops=4 * heads * src * vis * keys * width,
            bytes_accessed=2 * x.size + 4 * heads * src * vis * width,
            transcendentals=heads * src * vis * keys,
        ),
        name="attend",
    )(length, x)


def split2(x):
    hi = x.astype(BF)
    return hi, (x - hi.astype(F32)).astype(BF)


def split3(x):
    a = x.astype(BF)
    rest = x - a.astype(F32)
    b = rest.astype(BF)
    return a, b, (rest - b.astype(F32)).astype(BF)


def places(cols, vis, patch):
    rows = 2 * patch + 16
    hidden, tables = [], []
    for k in range(4):
        at, across = (k // 2) * vis, (k % 2) * 4 * cols
        hidden.append((slice(at, at + vis), slice(across, across + 4 * cols)))
        at, across = (k // 2) * rows, 8 * cols + (k % 2) * (cols + 64)
        tables.append((slice(at, at + rows), slice(across, across + cols + 64)))
    return hidden, tables


def stage_kernel(mod_hbm, fin_hbm, *refs):
    w_hbm, got_hbm, (aux_ref, out_hbm) = refs[:4], refs[4:8], refs[8:10]
    mod_ref, fin_ref, w_ref, sem = refs[10:]
    core, row, col = (lax.axis_index(a) for a in ("cfg", "row", "col"))
    part, vis = w_hbm[0].shape[0], got_hbm[0].shape[0]
    patch = fin_ref.shape[0]
    hidden, tables = places(part, vis, patch)
    loads = [
        pltpu.make_async_copy(mod_hbm.at[0], mod_ref, sem.at[0]),
        pltpu.make_async_copy(fin_hbm, fin_ref, sem.at[1]),
    ]
    moves = [
        pltpu.make_async_copy(w_hbm[g], w_ref.at[g * part : (g + 1) * part], sem.at[2 + g])
        for g in range(4)
    ]
    for load in loads + moves:
        load.start()
    for load in loads:
        load.wait()
    for me in range(4):

        @pl.when(col == me)
        def _():
            copies = [
                pltpu.make_async_copy(got_hbm[d], aux_ref.at[hidden[me ^ d]], sem.at[6 + d])
                for d in range(4)
            ]
            for copy in copies:
                copy.start()
            own = slice(me * part, (me + 1) * part)
            total, shift = 0.0, 0.0
            for g, window in enumerate(windows(core, row, 4 * part)):
                f = fin_ref[:, window].astype(F32)[:, own]
                scaled = f * (1.0 + mod_ref[1:2, window][:, own])
                total = total + jnp.sum(scaled, axis=1, keepdims=True)
                moved = f * mod_ref[2:3, window][:, own]
                shift = shift + jnp.sum(moved, axis=1, keepdims=True)
                hi, lo = split2(scaled)
                gate = split3(jnp.broadcast_to(mod_ref[0:1, window][:, own], (16, part)))
                line = lax.broadcasted_iota(jnp.int32, (16, part), 0)
                gate = jnp.where(line == 0, gate[0], jnp.where(line == 1, gate[1], gate[2]))
                both = jnp.concatenate([hi, lo, gate], axis=0)
                extra = jnp.zeros((both.shape[0], 64), BF)
                if g == 3:
                    lane = lax.broadcasted_iota(jnp.int32, (patch, 64), 1)
                    pieces = split3(jnp.where(lane % 2 == 0, total, shift))
                    pieces = jnp.where(
                        lane < 2, pieces[0], jnp.where(lane < 4, pieces[1], pieces[2])
                    )
                    extra = jnp.concatenate([pieces, extra[patch:]], axis=0)
                aux_ref[tables[g]] = jnp.concatenate([both, extra], axis=1)
            for copy in copies:
                copy.wait()

    for move in moves:
        move.wait()
    store = pltpu.make_async_copy(w_ref, out_hbm, sem.at[0])
    store.start()
    store.wait()


def stage(modulation, final_t, blocks, got):
    patch, width = final_t.shape
    cols, depth = blocks[0].shape
    rows = 2 * max(got[0].shape[0], 2 * patch + 16)
    return pl.pallas_call(
        stage_kernel,
        in_specs=[ANY] * 10,
        out_specs=[WHOLE, ANY],
        out_shape=[
            jax.ShapeDtypeStruct((rows, depth), BF),
            jax.ShapeDtypeStruct((4 * cols, depth), BF),
        ],
        scratch_shapes=[
            pltpu.VMEM(modulation.shape[1:], F32),
            pltpu.VMEM(final_t.shape, BF),
            pltpu.VMEM((4 * cols, depth), BF),
            pltpu.SemaphoreType.DMA((10,)),
        ],
        compiler_params=pltpu.CompilerParams(vmem_limit_bytes=STAGE),
        cost_estimate=pl.CostEstimate(flops=2 * 10**10, bytes_accessed=0, transcendentals=0),
        name="stage",
    )(modulation, final_t, *blocks, *got)


def project_kernel(a_ref, aux_ref, w_hbm, o_ref, w_ref, r_ref, sem):
    chunks, tokens, depth = a_ref.shape
    part = r_ref.shape[2]
    vis, patch = tokens // 4, 2 * o_ref.shape[1] - 16
    hidden, tables = places(part, vis, patch)
    loads = []
    for g in range(4):
        at = slice(g * part, (g + 1) * part)
        loads.append(pltpu.make_async_copy(w_hbm.at[at], w_ref.at[at], sem.at[g]))
        loads[g].start()
    for g in range(4):
        for k, (rows, c) in enumerate(hidden):
            h = aux_ref[rows, c.start + g * part : c.start + (g + 1) * part]
            r_ref[g, k * vis : (k + 1) * vis, :] = h.astype(F32)
    lhs = jnp.concatenate([a_ref[i] for i in range(chunks)], axis=1)
    for load in loads:
        load.wait()
    total = 0.0
    for g in range(4):
        w = w_ref[g * part : (g + 1) * part, :]
        p = lax.dot_general(lhs, w, NT, preferred_element_type=F32)
        rows, c = tables[g]
        gate = aux_ref[rows.start + 2 * patch : rows.stop, c.start : c.start + part].astype(F32)
        r = r_ref[g] + (gate[0:1] + gate[1:2] + gate[2:3]) * p
        r_ref[g] = r
        total = total + r
    mean = jnp.sum(total, axis=1, keepdims=True) * (1.0 / (4 * part))
    spread, both, fine = 0.0, 0.0, 0.0
    for g in range(4):
        d = r_ref[g] - mean
        spread = spread + d * d
        hi, lo = split2(d)
        rows, c = tables[g]
        w = aux_ref[rows.start : rows.start + 2 * patch, c.start : c.start + part]
        both = both + lax.dot_general(hi, w, NT, preferred_element_type=F32)
        fine = fine + lax.dot_general(lo, w[:patch], NT, preferred_element_type=F32)
    pred = both[:, :patch] + both[:, patch:] + fine
    stats = [mean, jnp.sum(spread, axis=1, keepdims=True), jnp.zeros((tokens, 78), F32)]
    pred = jnp.transpose(jnp.concatenate([pred, *stats], axis=1))
    rows, c = tables[3]
    sums = aux_ref[rows.start : rows.start + patch, c.start + part : c.stop].astype(F32)
    sums = (sums[:, :32] + sums[:, 2:34]) + sums[:, 4:36]
    half = patch // 2
    for core in range(2):
        for k in range(4):
            at = slice(k * vis, (k + 1) * vis)
            rows = slice(core * half, (core + 1) * half)
            o_ref[core * 4 + k, :half] = jnp.concatenate([pred[rows, at], sums[rows]], axis=1)
            o_ref[core * 4 + k, half:] = jnp.concatenate(
                [pred[patch : patch + 8, at], sums[:8]], axis=1
            )


def project(att, aux, weights, patch):
    chunks, tokens, width = att.shape
    depth = chunks * width
    cols = weights.shape[0] // 4
    return pl.pallas_call(
        project_kernel,
        in_specs=[WHOLE, WHOLE, ANY],
        out_specs=WHOLE,
        out_shape=jax.ShapeDtypeStruct((8, patch // 2 + 8, 128), F32),
        scratch_shapes=[
            pltpu.VMEM(weights.shape, BF),
            pltpu.VMEM((4, tokens, cols), F32),
            pltpu.SemaphoreType.DMA((4,)),
        ],
        compiler_params=pltpu.CompilerParams(vmem_limit_bytes=MOST),
        cost_estimate=pl.CostEstimate(
            flops=8 * cols * depth * tokens,
            bytes_accessed=8 * cols * depth,
            transcendentals=0,
        ),
        name="project",
    )(att, aux, weights)


def update_kernel(step_ref, x_ref, lat_ref, vel_ref, next_ref, den_ref, *, count):
    half, vis = lat_ref.shape
    preds = []
    for b in range(2):
        parts = [x_ref[b * 4 + k] for k in range(4)]
        means = [t[half : half + 1, :vis] for t in parts]
        mean = 0.25 * (means[0] + means[1] + means[2] + means[3])
        spread, linear, shift = 0.0, 0.0, 0.0
        for k in range(4):
            off = means[k] - mean
            spread = spread + parts[k][half + 1 : half + 2, :vis] + (0.25 * count) * (off * off)
            linear = linear + parts[k][:half, :vis] + parts[k][:half, vis : vis + 1] * off
            shift = shift + parts[k][:half, vis + 1 : vis + 2]
        preds.append(linear * lax.rsqrt(spread * (1.0 / count) + 1e-06) + shift)
    cond, uncond = preds
    velocity = uncond + 4.5 * (cond - uncond)
    step_now = step_ref[0].astype(F32)
    remain_now = 1.0 - step_now * (1.0 / STEPS)
    remain_next = 1.0 - (step_now + 1.0) * (1.0 / STEPS)
    sigma_now = remain_now * remain_now
    sigma_next = remain_next * remain_next
    latent = lat_ref[...]
    vel_ref[...] = velocity
    next_ref[...] = latent + (sigma_next - sigma_now) * velocity
    den_ref[...] = latent - sigma_now * velocity


def update(timestep, parts, latent, count):
    return pl.pallas_call(
        functools.partial(update_kernel, count=count),
        in_specs=[SCALARS, WHOLE, WHOLE],
        out_specs=[WHOLE] * 3,
        out_shape=[jax.ShapeDtypeStruct(latent.shape, F32)] * 3,
        compiler_params=pltpu.CompilerParams(vmem_limit_bytes=2 << 20),
        name="update",
    )(timestep, parts, latent)


def across_outer(reqs):
    deep = 8
    if reqs % deep:
        return None
    high = reqs // deep
    pairs = []
    for r in range(reqs):
        for s in range(8):
            y = 2 * (r // deep) + s // 4
            near = (y + 1 if y % 2 else y - 1) % (2 * high)
            pairs.append((r * 8 + s, (near // 2 * deep + r % deep) * 8 + near % 2 * 4 + s % 4))
    return pairs


def shards(
    vis_qkv, text_kv, text_len, vis_hidden, out_weight, modulation, final_weight, latent, timestep
):
    vis, txt = vis_qkv.shape[1], text_kv.shape[1]
    cores = [(0, 1), (1, 0)]
    outer = across_outer(lax.axis_size("req"))

    own = out_weight.T

    def across(block):
        if outer is None:
            return lax.ppermute(block, "row", cores)
        return lax.ppermute(block, ("req", "row", "col"), outer)

    far = across(own)
    packed, hidden = lax.optimization_barrier((pack(vis_qkv, text_kv), vis_hidden))
    mine, *sends = share(hidden)
    heads = lax.all_to_all(
        packed, ("row", "col"), split_axis=0, concat_axis=0, tiled=True
    ).reshape(8, 2, 3 * vis + 2 * txt, 128)
    got = [mine] + [
        lax.ppermute(block, "col", [(c, c ^ d) for c in range(4)])
        for d, block in zip((1, 2, 3), sends)
    ]
    attended = attend(text_len[0], heads, vis)
    far, modulation, *got = lax.optimization_barrier((far, modulation, *got))
    own_other, far_other = (lax.ppermute(b, "cfg", cores) for b in (own, far))
    aux, weights = stage(modulation, final_weight.T, [own, far, own_other, far_other], got)
    att = lax.all_to_all(
        attended, ("row", "col"), split_axis=0, concat_axis=0, tiled=True
    ).reshape(16, 4 * vis, 128)
    parts = project(att, aux, weights, final_weight.shape[1])
    parts = lax.all_to_all(parts, ("cfg", "col"), split_axis=0, concat_axis=0, tiled=True)
    outs = update(timestep, parts, latent.T, vis_hidden.shape[2])
    return tuple(o.T for o in outs)


def solution(mesh):
    req, cfg, sp = mesh.devices.shape
    fine = jax.sharding.Mesh(
        mesh.devices.reshape(req, cfg, 2, sp // 2), ("req", "cfg", "row", "col")
    )
    tokens = ("req", "row", "col")
    out = P(tokens, "cfg")
    return jax.shard_map(
        shards,
        mesh=fine,
        in_specs=(
            P("cfg", tokens, None, None, None),
            P("cfg", tokens, None, None, None),
            P("cfg", "req"),
            P("cfg", tokens, None),
            P(None, ("cfg", "row", "col")),
            P("cfg", "req", None),
            P(),
            out,
            P("req"),
        ),
        out_specs=(out, out, out),
        check_vma=False,
    )
```

```python
import functools
import math

import jax
import jax.numpy as jnp
from jax import lax
from jax.experimental import pallas as pl
from jax.experimental.pallas import tpu as pltpu
from jax.sharding import PartitionSpec as P

STEPS = 64
SMALL = 16 << 20
LARGE = 56 << 20
MOST = 51 << 20
STAGE = 10 << 20
NEG = -1e30
BF = jnp.bfloat16
F32 = jnp.float32
ANY = pl.BlockSpec(memory_space=pltpu.HBM)
WHOLE = pl.BlockSpec(memory_space=pltpu.VMEM)
SCALARS = pl.BlockSpec(memory_space=pltpu.SMEM)
NT = (((1,), (1,)), ((), ()))


def windows(core, row, width):
    starts = []
    for c in (core, 1 - core):
        for r in (row, 1 - row):
            starts.append(pl.ds(pl.multiple_of((2 * c + r) * width, 128), width))
    return starts


def pack_kernel(vis_ref, txt_ref, o_ref, v_ref, t_ref, out_ref, in_sem, out_sem):
    vis, txt = v_ref.shape[1], t_ref.shape[1]
    loads = [
        pltpu.make_async_copy(vis_ref.at[0, :, j], v_ref.at[j], in_sem.at[j]) for j in range(3)
    ] + [
        pltpu.make_async_copy(txt_ref.at[0, :, j], t_ref.at[j], in_sem.at[3 + j]) for j in range(2)
    ]
    for load in loads:
        load.start()
    stores = []
    at = 0
    for j in range(5):
        loads[j].wait()
        block = v_ref[j] if j < 3 else t_ref[j - 3]
        rows = vis if j < 3 else txt
        out_ref[:, at : at + rows, :] = jnp.swapaxes(block, 0, 1)
        stores.append(
            pltpu.make_async_copy(
                out_ref.at[:, at : at + rows, :], o_ref.at[:, at : at + rows, :], out_sem.at[j]
            )
        )
        stores[-1].start()
        at += rows
    for store in stores:
        store.wait()


def pack(vis_qkv, text_kv):
    _, vis, _, heads, width = vis_qkv.shape
    txt = text_kv.shape[1]
    rows = 3 * vis + 2 * txt
    return pl.pallas_call(
        pack_kernel,
        in_specs=[ANY, ANY],
        out_specs=ANY,
        out_shape=jax.ShapeDtypeStruct((heads, rows, width), BF),
        scratch_shapes=[
            pltpu.VMEM((3, vis, heads, width), BF),
            pltpu.VMEM((2, txt, heads, width), BF),
            pltpu.VMEM((heads, rows, width), BF),
            pltpu.SemaphoreType.DMA((5,)),
            pltpu.SemaphoreType.DMA((5,)),
        ],
        compiler_params=pltpu.CompilerParams(vmem_limit_bytes=LARGE),
        cost_estimate=pl.CostEstimate(
            flops=0, bytes_accessed=4 * heads * rows * width, transcendentals=0
        ),
        name="pack",
    )(vis_qkv, text_kv)


def share_kernel(hid_hbm, *refs):
    sends, (hid_ref, sem) = refs[:4], refs[4:]
    load = pltpu.make_async_copy(hid_hbm.at[0], hid_ref, sem)
    load.start()
    core, row, col = (lax.axis_index(a) for a in ("cfg", "row", "col"))
    part = sends[0].shape[1] // 4
    load.wait()
    for me in range(4):

        @pl.when(col == me)
        def _():
            for g, window in enumerate(windows(core, row, 4 * part)):
                hid = hid_ref[:, window]
                for d in range(4):
                    there = me ^ d
                    at = slice(there * part, (there + 1) * part)
                    sends[d][:, g * part : (g + 1) * part] = hid[:, at]


def share(hidden):
    _, vis, width = hidden.shape
    return pl.pallas_call(
        share_kernel,
        in_specs=[ANY],
        out_specs=[WHOLE] * 4,
        out_shape=[jax.ShapeDtypeStruct((vis, width // 4), BF)] * 4,
        scratch_shapes=[pltpu.VMEM((vis, width), BF), pltpu.SemaphoreType.DMA],
        compiler_params=pltpu.CompilerParams(vmem_limit_bytes=LARGE),
        name="share",
    )(hidden)


def attend_kernel(len_ref, x_ref, o_hbm, k_ref, v_ref, o_ref, sem):
    src, heads, rows, width = x_ref.shape
    cols = src // 2
    vis = o_ref.shape[2] // 2
    txt = (rows - 3 * vis) // 2
    nv = src * vis
    keys = k_ref.shape[1]
    valid = lax.broadcasted_iota(jnp.int32, (1, keys - nv), 1) < len_ref[0]
    scale = math.log2(math.e) / math.sqrt(width)
    ones = jnp.ones((keys, width), BF)
    stores = []
    for h in range(heads):
        for i in range(src):
            at, t0 = slice(i * vis, (i + 1) * vis), nv + i * txt
            k_ref[h, at, :] = x_ref[i, h, vis : 2 * vis, :]
            v_ref[h, at, :width] = x_ref[i, h, 2 * vis : 3 * vis, :]
            k_ref[h, t0 : t0 + txt, :] = x_ref[i, h, 3 * vis : 3 * vis + txt, :]
            v_ref[h, t0 : t0 + txt, :width] = x_ref[i, h, 3 * vis + txt : 3 * vis + 2 * txt, :]
        v_ref[h, :, width:] = ones
        for i in range(0, src, 2):
            q = jnp.concatenate([x_ref[i, h, 0:vis, :], x_ref[i + 1, h, 0:vis, :]], axis=0)
            s = lax.dot_general(q, k_ref[h], NT, preferred_element_type=F32)
            s = jnp.concatenate([s[:, :nv], jnp.where(valid, s[:, nv:], NEG)], axis=1)
            e = jnp.exp2((s - jnp.max(s, axis=1, keepdims=True)) * scale)
            o = jnp.dot(e.astype(BF), v_ref[h], preferred_element_type=F32)
            n = h * src + i
            o_ref[h, i // 2] = (o[:, :width] / o[:, width:]).astype(BF)
            row, at = i // cols, (i % cols) * vis
            for d in range(row * cols, (row + 1) * cols):
                stores.append(
                    pltpu.make_async_copy(
                        o_ref.at[h, i // 2], o_hbm.at[d, h, pl.ds(at, 2 * vis)], sem.at[n + d % 2]
                    )
                )
                stores[-1].start()
    for store in stores:
        store.wait()


def attend(length, x, vis):
    src, heads, rows, width = x.shape
    txt = (rows - 3 * vis) // 2
    keys = src * (vis + txt)
    return pl.pallas_call(
        attend_kernel,
        in_specs=[SCALARS, WHOLE],
        out_specs=ANY,
        out_shape=jax.ShapeDtypeStruct((src, heads, src // 2 * vis, width), BF),
        scratch_shapes=[
            pltpu.VMEM((heads, keys, width), BF),
            pltpu.VMEM((heads, keys, 2 * width), BF),
            pltpu.VMEM((heads, src // 2, 2 * vis, width), BF),
            pltpu.SemaphoreType.DMA((heads * src,)),
        ],
        compiler_params=pltpu.CompilerParams(vmem_limit_bytes=SMALL),
        cost_estimate=pl.CostEstimate(
            flops=4 * heads * src * vis * keys * width,
            bytes_accessed=2 * x.size + 4 * heads * src * vis * width,
            transcendentals=heads * src * vis * keys,
        ),
        name="attend",
    )(length, x)


def split2(x):
    hi = x.astype(BF)
    return hi, (x - hi.astype(F32)).astype(BF)


def split3(x):
    a = x.astype(BF)
    rest = x - a.astype(F32)
    b = rest.astype(BF)
    return a, b, (rest - b.astype(F32)).astype(BF)


def places(cols, vis, patch):
    rows = 2 * patch + 16
    hidden, tables = [], []
    for k in range(4):
        at, across = (k // 2) * vis, (k % 2) * 4 * cols
        hidden.append((slice(at, at + vis), slice(across, across + 4 * cols)))
        at, across = (k // 2) * rows, 8 * cols + (k % 2) * (cols + 64)
        tables.append((slice(at, at + rows), slice(across, across + cols + 64)))
    return hidden, tables


def stage_kernel(mod_hbm, fin_hbm, *refs):
    w_hbm, got_hbm, (aux_ref, out_hbm) = refs[:4], refs[4:8], refs[8:10]
    mod_ref, fin_ref, w_ref, sem = refs[10:]
    core, row, col = (lax.axis_index(a) for a in ("cfg", "row", "col"))
    part, vis = w_hbm[0].shape[0], got_hbm[0].shape[0]
    patch = fin_ref.shape[0]
    hidden, tables = places(part, vis, patch)
    loads = [
        pltpu.make_async_copy(mod_hbm.at[0], mod_ref, sem.at[0]),
        pltpu.make_async_copy(fin_hbm, fin_ref, sem.at[1]),
    ]
    moves = [
        pltpu.make_async_copy(w_hbm[g], w_ref.at[g * part : (g + 1) * part], sem.at[2 + g])
        for g in range(4)
    ]
    for load in loads + moves:
        load.start()
    for load in loads:
        load.wait()
    for me in range(4):

        @pl.when(col == me)
        def _():
            copies = [
                pltpu.make_async_copy(got_hbm[d], aux_ref.at[hidden[me ^ d]], sem.at[6 + d])
                for d in range(4)
            ]
            for copy in copies:
                copy.start()
            own = slice(me * part, (me + 1) * part)
            total, shift = 0.0, 0.0
            for g, window in enumerate(windows(core, row, 4 * part)):
                f = fin_ref[:, window].astype(F32)[:, own]
                scaled = f * (1.0 + mod_ref[1:2, window][:, own])
                total = total + jnp.sum(scaled, axis=1, keepdims=True)
                moved = f * mod_ref[2:3, window][:, own]
                shift = shift + jnp.sum(moved, axis=1, keepdims=True)
                hi, lo = split2(scaled)
                gate = split3(jnp.broadcast_to(mod_ref[0:1, window][:, own], (16, part)))
                line = lax.broadcasted_iota(jnp.int32, (16, part), 0)
                gate = jnp.where(line == 0, gate[0], jnp.where(line == 1, gate[1], gate[2]))
                both = jnp.concatenate([hi, lo, gate], axis=0)
                extra = jnp.zeros((both.shape[0], 64), BF)
                if g == 3:
                    lane = lax.broadcasted_iota(jnp.int32, (patch, 64), 1)
                    pieces = split3(jnp.where(lane % 2 == 0, total, shift))
                    pieces = jnp.where(
                        lane < 2, pieces[0], jnp.where(lane < 4, pieces[1], pieces[2])
                    )
                    extra = jnp.concatenate([pieces, extra[patch:]], axis=0)
                aux_ref[tables[g]] = jnp.concatenate([both, extra], axis=1)
            for copy in copies:
                copy.wait()

    for move in moves:
        move.wait()
    store = pltpu.make_async_copy(w_ref, out_hbm, sem.at[0])
    store.start()
    store.wait()


def stage(modulation, final_t, blocks, got):
    patch, width = final_t.shape
    cols, depth = blocks[0].shape
    rows = 2 * max(got[0].shape[0], 2 * patch + 16)
    return pl.pallas_call(
        stage_kernel,
        in_specs=[ANY] * 10,
        out_specs=[WHOLE, ANY],
        out_shape=[
            jax.ShapeDtypeStruct((rows, depth), BF),
            jax.ShapeDtypeStruct((4 * cols, depth), BF),
        ],
        scratch_shapes=[
            pltpu.VMEM(modulation.shape[1:], F32),
            pltpu.VMEM(final_t.shape, BF),
            pltpu.VMEM((4 * cols, depth), BF),
            pltpu.SemaphoreType.DMA((10,)),
        ],
        compiler_params=pltpu.CompilerParams(vmem_limit_bytes=STAGE),
        cost_estimate=pl.CostEstimate(flops=2 * 10**10, bytes_accessed=0, transcendentals=0),
        name="stage",
    )(modulation, final_t, *blocks, *got)


def project_kernel(a_ref, aux_ref, w_hbm, o_ref, w_ref, r_ref, sem):
    chunks, tokens, depth = a_ref.shape
    part = r_ref.shape[2]
    vis, patch = tokens // 4, 2 * o_ref.shape[1] - 16
    hidden, tables = places(part, vis, patch)
    loads = []
    for g in range(4):
        at = slice(g * part, (g + 1) * part)
        loads.append(pltpu.make_async_copy(w_hbm.at[at], w_ref.at[at], sem.at[g]))
        loads[g].start()
    for g in range(4):
        for k, (rows, c) in enumerate(hidden):
            h = aux_ref[rows, c.start + g * part : c.start + (g + 1) * part]
            r_ref[g, k * vis : (k + 1) * vis, :] = h.astype(F32)
    lhs = jnp.concatenate([a_ref[i] for i in range(chunks)], axis=1)
    total = 0.0
    for g in range(4):
        if g % 2 == 0:
            loads[g].wait()
            loads[g + 1].wait()
        w = w_ref[g * part : (g + 1) * part, :]
        p = lax.dot_general(lhs, w, NT, preferred_element_type=F32)
        rows, c = tables[g]
        gate = aux_ref[rows.start + 2 * patch : rows.stop, c.start : c.start + part].astype(F32)
        r = r_ref[g] + (gate[0:1] + gate[1:2] + gate[2:3]) * p
        r_ref[g] = r
        total = total + r
    mean = jnp.sum(total, axis=1, keepdims=True) * (1.0 / (4 * part))
    spread, both, fine = 0.0, 0.0, 0.0
    for g in range(4):
        d = r_ref[g] - mean
        spread = spread + d * d
        hi, lo = split2(d)
        rows, c = tables[g]
        w = aux_ref[rows.start : rows.start + 2 * patch, c.start : c.start + part]
        both = both + lax.dot_general(hi, w, NT, preferred_element_type=F32)
        fine = fine + lax.dot_general(lo, w[:patch], NT, preferred_element_type=F32)
    pred = both[:, :patch] + both[:, patch:] + fine
    stats = [mean, jnp.sum(spread, axis=1, keepdims=True), jnp.zeros((tokens, 78), F32)]
    pred = jnp.transpose(jnp.concatenate([pred, *stats], axis=1))
    rows, c = tables[3]
    sums = aux_ref[rows.start : rows.start + patch, c.start + part : c.stop].astype(F32)
    sums = (sums[:, :32] + sums[:, 2:34]) + sums[:, 4:36]
    half = patch // 2
    for core in range(2):
        for k in range(4):
            at = slice(k * vis, (k + 1) * vis)
            rows = slice(core * half, (core + 1) * half)
            o_ref[core * 4 + k, :half] = jnp.concatenate([pred[rows, at], sums[rows]], axis=1)
            o_ref[core * 4 + k, half:] = jnp.concatenate(
                [pred[patch : patch + 8, at], sums[:8]], axis=1
            )


def project(att, aux, weights, patch):
    chunks, tokens, width = att.shape
    depth = chunks * width
    cols = weights.shape[0] // 4
    return pl.pallas_call(
        project_kernel,
        in_specs=[WHOLE, WHOLE, ANY],
        out_specs=WHOLE,
        out_shape=jax.ShapeDtypeStruct((8, patch // 2 + 8, 128), F32),
        scratch_shapes=[
            pltpu.VMEM(weights.shape, BF),
            pltpu.VMEM((4, tokens, cols), F32),
            pltpu.SemaphoreType.DMA((4,)),
        ],
        compiler_params=pltpu.CompilerParams(vmem_limit_bytes=MOST),
        cost_estimate=pl.CostEstimate(
            flops=8 * cols * depth * tokens,
            bytes_accessed=8 * cols * depth,
            transcendentals=0,
        ),
        name="project",
    )(att, aux, weights)


def update_kernel(step_ref, x_ref, lat_ref, vel_ref, next_ref, den_ref, *, count):
    half, vis = lat_ref.shape
    preds = []
    for b in range(2):
        parts = [x_ref[b * 4 + k] for k in range(4)]
        means = [t[half : half + 1, :vis] for t in parts]
        mean = 0.25 * (means[0] + means[1] + means[2] + means[3])
        spread, linear, shift = 0.0, 0.0, 0.0
        for k in range(4):
            off = means[k] - mean
            spread = spread + parts[k][half + 1 : half + 2, :vis] + (0.25 * count) * (off * off)
            linear = linear + parts[k][:half, :vis] + parts[k][:half, vis : vis + 1] * off
            shift = shift + parts[k][:half, vis + 1 : vis + 2]
        preds.append(linear * lax.rsqrt(spread * (1.0 / count) + 1e-06) + shift)
    cond, uncond = preds
    velocity = uncond + 4.5 * (cond - uncond)
    step_now = step_ref[0].astype(F32)
    remain_now = 1.0 - step_now * (1.0 / STEPS)
    remain_next = 1.0 - (step_now + 1.0) * (1.0 / STEPS)
    sigma_now = remain_now * remain_now
    sigma_next = remain_next * remain_next
    latent = lat_ref[...]
    vel_ref[...] = velocity
    next_ref[...] = latent + (sigma_next - sigma_now) * velocity
    den_ref[...] = latent - sigma_now * velocity


def update(timestep, parts, latent, count):
    return pl.pallas_call(
        functools.partial(update_kernel, count=count),
        in_specs=[SCALARS, WHOLE, WHOLE],
        out_specs=[WHOLE] * 3,
        out_shape=[jax.ShapeDtypeStruct(latent.shape, F32)] * 3,
        compiler_params=pltpu.CompilerParams(vmem_limit_bytes=2 << 20),
        name="update",
    )(timestep, parts, latent)


def across_outer(reqs):
    deep = 8
    if reqs % deep:
        return None
    high = reqs // deep
    pairs = []
    for r in range(reqs):
        for s in range(8):
            y = 2 * (r // deep) + s // 4
            near = (y + 1 if y % 2 else y - 1) % (2 * high)
            pairs.append((r * 8 + s, (near // 2 * deep + r % deep) * 8 + near % 2 * 4 + s % 4))
    return pairs


def shards(
    vis_qkv, text_kv, text_len, vis_hidden, out_weight, modulation, final_weight, latent, timestep
):
    vis, txt = vis_qkv.shape[1], text_kv.shape[1]
    cores = [(0, 1), (1, 0)]
    outer = across_outer(lax.axis_size("req"))

    own = out_weight.T

    def across(block):
        if outer is None:
            return lax.ppermute(block, "row", cores)
        return lax.ppermute(block, ("req", "row", "col"), outer)

    far = across(own)
    packed, hidden = lax.optimization_barrier((pack(vis_qkv, text_kv), vis_hidden))
    mine, *sends = share(hidden)
    heads = lax.all_to_all(
        packed, ("row", "col"), split_axis=0, concat_axis=0, tiled=True
    ).reshape(8, 2, 3 * vis + 2 * txt, 128)
    got = [mine] + [
        lax.ppermute(block, "col", [(c, c ^ d) for c in range(4)])
        for d, block in zip((1, 2, 3), sends)
    ]
    attended = attend(text_len[0], heads, vis)
    far, modulation, *got = lax.optimization_barrier((far, modulation, *got))
    own_other, far_other = (lax.ppermute(b, "cfg", cores) for b in (own, far))
    aux, weights = stage(modulation, final_weight.T, [own, far, own_other, far_other], got)
    att = lax.all_to_all(
        attended, ("row", "col"), split_axis=0, concat_axis=0, tiled=True
    ).reshape(16, 4 * vis, 128)
    parts = project(att, aux, weights, final_weight.shape[1])
    parts = lax.all_to_all(parts, ("cfg", "col"), split_axis=0, concat_axis=0, tiled=True)
    outs = update(timestep, parts, latent.T, vis_hidden.shape[2])
    return tuple(o.T for o in outs)


def solution(mesh):
    req, cfg, sp = mesh.devices.shape
    fine = jax.sharding.Mesh(
        mesh.devices.reshape(req, cfg, 2, sp // 2), ("req", "cfg", "row", "col")
    )
    tokens = ("req", "row", "col")
    out = P(tokens, "cfg")
    return jax.shard_map(
        shards,
        mesh=fine,
        in_specs=(
            P("cfg", tokens, None, None, None),
            P("cfg", tokens, None, None, None),
            P("cfg", "req"),
            P("cfg", tokens, None),
            P(None, ("cfg", "row", "col")),
            P("cfg", "req", None),
            P(),
            out,
            P("req"),
        ),
        out_specs=(out, out, out),
        check_vma=False,
    )
```

```python
import functools
import math

import jax
import jax.numpy as jnp
from jax import lax
from jax.experimental import pallas as pl
from jax.experimental.pallas import tpu as pltpu
from jax.sharding import PartitionSpec as P

STEPS = 64
SMALL = 16 << 20
LARGE = 56 << 20
MOST = 51 << 20
STAGE = 10 << 20
NEG = -1e30
BF = jnp.bfloat16
F32 = jnp.float32
ANY = pl.BlockSpec(memory_space=pltpu.HBM)
WHOLE = pl.BlockSpec(memory_space=pltpu.VMEM)
SCALARS = pl.BlockSpec(memory_space=pltpu.SMEM)
NT = (((1,), (1,)), ((), ()))


def windows(core, row, width):
    starts = []
    for c in (core, 1 - core):
        for r in (row, 1 - row):
            starts.append(pl.ds(pl.multiple_of((2 * c + r) * width, 128), width))
    return starts


def pack_kernel(vis_ref, txt_ref, o_ref, v_ref, t_ref, out_ref, in_sem, out_sem):
    vis, txt = v_ref.shape[1], t_ref.shape[1]
    loads = [
        pltpu.make_async_copy(vis_ref.at[0, :, j], v_ref.at[j], in_sem.at[j]) for j in range(3)
    ] + [
        pltpu.make_async_copy(txt_ref.at[0, :, j], t_ref.at[j], in_sem.at[3 + j]) for j in range(2)
    ]
    for load in loads:
        load.start()
    stores = []
    at = 0
    for j in range(5):
        loads[j].wait()
        block = v_ref[j] if j < 3 else t_ref[j - 3]
        rows = vis if j < 3 else txt
        out_ref[:, at : at + rows, :] = jnp.swapaxes(block, 0, 1)
        stores.append(
            pltpu.make_async_copy(
                out_ref.at[:, at : at + rows, :], o_ref.at[:, at : at + rows, :], out_sem.at[j]
            )
        )
        stores[-1].start()
        at += rows
    for store in stores:
        store.wait()


def pack(vis_qkv, text_kv):
    _, vis, _, heads, width = vis_qkv.shape
    txt = text_kv.shape[1]
    rows = 3 * vis + 2 * txt
    return pl.pallas_call(
        pack_kernel,
        in_specs=[ANY, ANY],
        out_specs=ANY,
        out_shape=jax.ShapeDtypeStruct((heads, rows, width), BF),
        scratch_shapes=[
            pltpu.VMEM((3, vis, heads, width), BF),
            pltpu.VMEM((2, txt, heads, width), BF),
            pltpu.VMEM((heads, rows, width), BF),
            pltpu.SemaphoreType.DMA((5,)),
            pltpu.SemaphoreType.DMA((5,)),
        ],
        compiler_params=pltpu.CompilerParams(vmem_limit_bytes=LARGE),
        cost_estimate=pl.CostEstimate(
            flops=0, bytes_accessed=4 * heads * rows * width, transcendentals=0
        ),
        name="pack",
    )(vis_qkv, text_kv)


def share_kernel(hid_hbm, *refs):
    sends, (hid_ref, sem) = refs[:4], refs[4:]
    load = pltpu.make_async_copy(hid_hbm.at[0], hid_ref, sem)
    load.start()
    core, row, col = (lax.axis_index(a) for a in ("cfg", "row", "col"))
    part = sends[0].shape[1] // 4
    load.wait()
    for me in range(4):

        @pl.when(col == me)
        def _():
            for g, window in enumerate(windows(core, row, 4 * part)):
                hid = hid_ref[:, window]
                for d in range(4):
                    there = me ^ d
                    at = slice(there * part, (there + 1) * part)
                    sends[d][:, g * part : (g + 1) * part] = hid[:, at]


def share(hidden):
    _, vis, width = hidden.shape
    return pl.pallas_call(
        share_kernel,
        in_specs=[ANY],
        out_specs=[WHOLE] * 4,
        out_shape=[jax.ShapeDtypeStruct((vis, width // 4), BF)] * 4,
        scratch_shapes=[pltpu.VMEM((vis, width), BF), pltpu.SemaphoreType.DMA],
        compiler_params=pltpu.CompilerParams(vmem_limit_bytes=STAGE),
        name="share",
    )(hidden)


def attend_kernel(len_ref, x_ref, o_hbm, k_ref, v_ref, o_ref, sem):
    src, heads, rows, width = x_ref.shape
    cols = src // 2
    vis = o_ref.shape[2] // 2
    txt = (rows - 3 * vis) // 2
    nv = src * vis
    keys = k_ref.shape[1]
    valid = lax.broadcasted_iota(jnp.int32, (1, keys - nv), 1) < len_ref[0]
    scale = math.log2(math.e) / math.sqrt(width)
    ones = jnp.ones((keys, width), BF)
    stores = []
    for h in range(heads):
        for i in range(src):
            at, t0 = slice(i * vis, (i + 1) * vis), nv + i * txt
            k_ref[h, at, :] = x_ref[i, h, vis : 2 * vis, :]
            v_ref[h, at, :width] = x_ref[i, h, 2 * vis : 3 * vis, :]
            k_ref[h, t0 : t0 + txt, :] = x_ref[i, h, 3 * vis : 3 * vis + txt, :]
            v_ref[h, t0 : t0 + txt, :width] = x_ref[i, h, 3 * vis + txt : 3 * vis + 2 * txt, :]
        v_ref[h, :, width:] = ones
        for i in range(0, src, 2):
            q = jnp.concatenate([x_ref[i, h, 0:vis, :], x_ref[i + 1, h, 0:vis, :]], axis=0)
            s = lax.dot_general(q, k_ref[h], NT, preferred_element_type=F32)
            s = jnp.concatenate([s[:, :nv], jnp.where(valid, s[:, nv:], NEG)], axis=1)
            e = jnp.exp2((s - jnp.max(s, axis=1, keepdims=True)) * scale)
            o = jnp.dot(e.astype(BF), v_ref[h], preferred_element_type=F32)
            n = h * src + i
            o_ref[h, i // 2] = (o[:, :width] / o[:, width:]).astype(BF)
            row, at = i // cols, (i % cols) * vis
            for d in range(row * cols, (row + 1) * cols):
                stores.append(
                    pltpu.make_async_copy(
                        o_ref.at[h, i // 2], o_hbm.at[d, h, pl.ds(at, 2 * vis)], sem.at[n + d % 2]
                    )
                )
                stores[-1].start()
    for store in stores:
        store.wait()


def attend(length, x, vis):
    src, heads, rows, width = x.shape
    txt = (rows - 3 * vis) // 2
    keys = src * (vis + txt)
    return pl.pallas_call(
        attend_kernel,
        in_specs=[SCALARS, WHOLE],
        out_specs=ANY,
        out_shape=jax.ShapeDtypeStruct((src, heads, src // 2 * vis, width), BF),
        scratch_shapes=[
            pltpu.VMEM((heads, keys, width), BF),
            pltpu.VMEM((heads, keys, 2 * width), BF),
            pltpu.VMEM((heads, src // 2, 2 * vis, width), BF),
            pltpu.SemaphoreType.DMA((heads * src,)),
        ],
        compiler_params=pltpu.CompilerParams(vmem_limit_bytes=SMALL),
        cost_estimate=pl.CostEstimate(
            flops=4 * heads * src * vis * keys * width,
            bytes_accessed=2 * x.size + 4 * heads * src * vis * width,
            transcendentals=heads * src * vis * keys,
        ),
        name="attend",
    )(length, x)


def split2(x):
    hi = x.astype(BF)
    return hi, (x - hi.astype(F32)).astype(BF)


def split3(x):
    a = x.astype(BF)
    rest = x - a.astype(F32)
    b = rest.astype(BF)
    return a, b, (rest - b.astype(F32)).astype(BF)


def places(cols, vis, patch):
    rows = 2 * patch + 16
    hidden, tables = [], []
    for k in range(4):
        at, across = (k // 2) * vis, (k % 2) * 4 * cols
        hidden.append((slice(at, at + vis), slice(across, across + 4 * cols)))
        at, across = (k // 2) * rows, 8 * cols + (k % 2) * (cols + 64)
        tables.append((slice(at, at + rows), slice(across, across + cols + 64)))
    return hidden, tables


def stage_kernel(mod_hbm, fin_hbm, *refs):
    w_hbm, got_hbm, (aux_ref, out_hbm) = refs[:4], refs[4:8], refs[8:10]
    mod_ref, fin_ref, w_ref, sem = refs[10:]
    core, row, col = (lax.axis_index(a) for a in ("cfg", "row", "col"))
    part, vis = w_hbm[0].shape[0], got_hbm[0].shape[0]
    patch = fin_ref.shape[0]
    hidden, tables = places(part, vis, patch)
    loads = [
        pltpu.make_async_copy(mod_hbm.at[0], mod_ref, sem.at[0]),
        pltpu.make_async_copy(fin_hbm, fin_ref, sem.at[1]),
    ]
    moves = [
        pltpu.make_async_copy(w_hbm[g], w_ref.at[g * part : (g + 1) * part], sem.at[2 + g])
        for g in range(4)
    ]
    for load in loads + moves:
        load.start()
    for load in loads:
        load.wait()
    for me in range(4):

        @pl.when(col == me)
        def _():
            copies = [
                pltpu.make_async_copy(got_hbm[d], aux_ref.at[hidden[me ^ d]], sem.at[6 + d])
                for d in range(4)
            ]
            for copy in copies:
                copy.start()
            own = slice(me * part, (me + 1) * part)
            total, shift = 0.0, 0.0
            for g, window in enumerate(windows(core, row, 4 * part)):
                f = fin_ref[:, window].astype(F32)[:, own]
                scaled = f * (1.0 + mod_ref[1:2, window][:, own])
                total = total + jnp.sum(scaled, axis=1, keepdims=True)
                moved = f * mod_ref[2:3, window][:, own]
                shift = shift + jnp.sum(moved, axis=1, keepdims=True)
                hi, lo = split2(scaled)
                gate = split3(jnp.broadcast_to(mod_ref[0:1, window][:, own], (16, part)))
                line = lax.broadcasted_iota(jnp.int32, (16, part), 0)
                gate = jnp.where(line == 0, gate[0], jnp.where(line == 1, gate[1], gate[2]))
                both = jnp.concatenate([hi, lo, gate], axis=0)
                extra = jnp.zeros((both.shape[0], 64), BF)
                if g == 3:
                    lane = lax.broadcasted_iota(jnp.int32, (patch, 64), 1)
                    pieces = split3(jnp.where(lane % 2 == 0, total, shift))
                    pieces = jnp.where(
                        lane < 2, pieces[0], jnp.where(lane < 4, pieces[1], pieces[2])
                    )
                    extra = jnp.concatenate([pieces, extra[patch:]], axis=0)
                aux_ref[tables[g]] = jnp.concatenate([both, extra], axis=1)
            for copy in copies:
                copy.wait()

    for move in moves:
        move.wait()
    store = pltpu.make_async_copy(w_ref, out_hbm, sem.at[0])
    store.start()
    store.wait()


def stage(modulation, final_t, blocks, got):
    patch, width = final_t.shape
    cols, depth = blocks[0].shape
    rows = 2 * max(got[0].shape[0], 2 * patch + 16)
    return pl.pallas_call(
        stage_kernel,
        in_specs=[ANY] * 10,
        out_specs=[WHOLE, ANY],
        out_shape=[
            jax.ShapeDtypeStruct((rows, depth), BF),
            jax.ShapeDtypeStruct((4 * cols, depth), BF),
        ],
        scratch_shapes=[
            pltpu.VMEM(modulation.shape[1:], F32),
            pltpu.VMEM(final_t.shape, BF),
            pltpu.VMEM((4 * cols, depth), BF),
            pltpu.SemaphoreType.DMA((10,)),
        ],
        compiler_params=pltpu.CompilerParams(vmem_limit_bytes=48 << 20),
        cost_estimate=pl.CostEstimate(flops=2 * 10**10, bytes_accessed=0, transcendentals=0),
        name="stage",
    )(modulation, final_t, *blocks, *got)


def project_kernel(a_ref, aux_ref, w_hbm, o_ref, w_ref, r_ref, sem):
    chunks, tokens, depth = a_ref.shape
    part = r_ref.shape[2]
    vis, patch = tokens // 4, 2 * o_ref.shape[1] - 16
    hidden, tables = places(part, vis, patch)
    loads = []
    for g in range(4):
        at = slice(g * part, (g + 1) * part)
        loads.append(pltpu.make_async_copy(w_hbm.at[at], w_ref.at[at], sem.at[g]))
        loads[g].start()
    for g in range(4):
        for k, (rows, c) in enumerate(hidden):
            h = aux_ref[rows, c.start + g * part : c.start + (g + 1) * part]
            r_ref[g, k * vis : (k + 1) * vis, :] = h.astype(F32)
    lhs = jnp.concatenate([a_ref[i] for i in range(chunks)], axis=1)
    total = 0.0
    for g in range(4):
        if g % 2 == 0:
            loads[g].wait()
            loads[g + 1].wait()
        w = w_ref[g * part : (g + 1) * part, :]
        p = lax.dot_general(lhs, w, NT, preferred_element_type=F32)
        rows, c = tables[g]
        gate = aux_ref[rows.start + 2 * patch : rows.stop, c.start : c.start + part].astype(F32)
        r = r_ref[g] + (gate[0:1] + gate[1:2] + gate[2:3]) * p
        r_ref[g] = r
        total = total + r
    mean = jnp.sum(total, axis=1, keepdims=True) * (1.0 / (4 * part))
    spread, both, fine = 0.0, 0.0, 0.0
    for g in range(4):
        d = r_ref[g] - mean
        spread = spread + d * d
        hi, lo = split2(d)
        rows, c = tables[g]
        w = aux_ref[rows.start : rows.start + 2 * patch, c.start : c.start + part]
        both = both + lax.dot_general(hi, w, NT, preferred_element_type=F32)
        fine = fine + lax.dot_general(lo, w[:patch], NT, preferred_element_type=F32)
    pred = both[:, :patch] + both[:, patch:] + fine
    stats = [mean, jnp.sum(spread, axis=1, keepdims=True), jnp.zeros((tokens, 78), F32)]
    pred = jnp.transpose(jnp.concatenate([pred, *stats], axis=1))
    rows, c = tables[3]
    sums = aux_ref[rows.start : rows.start + patch, c.start + part : c.stop].astype(F32)
    sums = (sums[:, :32] + sums[:, 2:34]) + sums[:, 4:36]
    half = patch // 2
    for core in range(2):
        for k in range(4):
            at = slice(k * vis, (k + 1) * vis)
            rows = slice(core * half, (core + 1) * half)
            o_ref[core * 4 + k, :half] = jnp.concatenate([pred[rows, at], sums[rows]], axis=1)
            o_ref[core * 4 + k, half:] = jnp.concatenate(
                [pred[patch : patch + 8, at], sums[:8]], axis=1
            )


def project(att, aux, weights, patch):
    chunks, tokens, width = att.shape
    depth = chunks * width
    cols = weights.shape[0] // 4
    return pl.pallas_call(
        project_kernel,
        in_specs=[WHOLE, WHOLE, ANY],
        out_specs=WHOLE,
        out_shape=jax.ShapeDtypeStruct((8, patch // 2 + 8, 128), F32),
        scratch_shapes=[
            pltpu.VMEM(weights.shape, BF),
            pltpu.VMEM((4, tokens, cols), F32),
            pltpu.SemaphoreType.DMA((4,)),
        ],
        compiler_params=pltpu.CompilerParams(vmem_limit_bytes=MOST),
        cost_estimate=pl.CostEstimate(
            flops=8 * cols * depth * tokens,
            bytes_accessed=8 * cols * depth,
            transcendentals=0,
        ),
        name="project",
    )(att, aux, weights)


def update_kernel(step_ref, x_ref, lat_ref, vel_ref, next_ref, den_ref, *, count):
    half, vis = lat_ref.shape
    preds = []
    for b in range(2):
        parts = [x_ref[b * 4 + k] for k in range(4)]
        means = [t[half : half + 1, :vis] for t in parts]
        mean = 0.25 * (means[0] + means[1] + means[2] + means[3])
        spread, linear, shift = 0.0, 0.0, 0.0
        for k in range(4):
            off = means[k] - mean
            spread = spread + parts[k][half + 1 : half + 2, :vis] + (0.25 * count) * (off * off)
            linear = linear + parts[k][:half, :vis] + parts[k][:half, vis : vis + 1] * off
            shift = shift + parts[k][:half, vis + 1 : vis + 2]
        preds.append(linear * lax.rsqrt(spread * (1.0 / count) + 1e-06) + shift)
    cond, uncond = preds
    velocity = uncond + 4.5 * (cond - uncond)
    step_now = step_ref[0].astype(F32)
    remain_now = 1.0 - step_now * (1.0 / STEPS)
    remain_next = 1.0 - (step_now + 1.0) * (1.0 / STEPS)
    sigma_now = remain_now * remain_now
    sigma_next = remain_next * remain_next
    latent = lat_ref[...]
    vel_ref[...] = velocity
    next_ref[...] = latent + (sigma_next - sigma_now) * velocity
    den_ref[...] = latent - sigma_now * velocity


def update(timestep, parts, latent, count):
    return pl.pallas_call(
        functools.partial(update_kernel, count=count),
        in_specs=[SCALARS, WHOLE, WHOLE],
        out_specs=[WHOLE] * 3,
        out_shape=[jax.ShapeDtypeStruct(latent.shape, F32)] * 3,
        compiler_params=pltpu.CompilerParams(vmem_limit_bytes=2 << 20),
        name="update",
    )(timestep, parts, latent)


def across_outer(reqs):
    deep = 8
    if reqs % deep:
        return None
    high = reqs // deep
    pairs = []
    for r in range(reqs):
        for s in range(8):
            y = 2 * (r // deep) + s // 4
            near = (y + 1 if y % 2 else y - 1) % (2 * high)
            pairs.append((r * 8 + s, (near // 2 * deep + r % deep) * 8 + near % 2 * 4 + s % 4))
    return pairs


def shards(
    vis_qkv, text_kv, text_len, vis_hidden, out_weight, modulation, final_weight, latent, timestep
):
    vis, txt = vis_qkv.shape[1], text_kv.shape[1]
    cores = [(0, 1), (1, 0)]
    outer = across_outer(lax.axis_size("req"))

    own = out_weight.T

    def across(block):
        if outer is None:
            return lax.ppermute(block, "row", cores)
        return lax.ppermute(block, ("req", "row", "col"), outer)

    far = across(own)
    packed, hidden = lax.optimization_barrier((pack(vis_qkv, text_kv), vis_hidden))
    mine, *sends = share(hidden)
    heads = lax.all_to_all(
        packed, ("row", "col"), split_axis=0, concat_axis=0, tiled=True
    ).reshape(8, 2, 3 * vis + 2 * txt, 128)
    got = [mine] + [
        lax.ppermute(block, "col", [(c, c ^ d) for c in range(4)])
        for d, block in zip((1, 2, 3), sends)
    ]
    attended = attend(text_len[0], heads, vis)
    far, modulation, *got = lax.optimization_barrier((far, modulation, *got))
    own_other, far_other = (lax.ppermute(b, "cfg", cores) for b in (own, far))
    aux, weights = stage(modulation, final_weight.T, [own, far, own_other, far_other], got)
    att = lax.all_to_all(
        attended, ("row", "col"), split_axis=0, concat_axis=0, tiled=True
    ).reshape(16, 4 * vis, 128)
    parts = project(att, aux, weights, final_weight.shape[1])
    parts = lax.all_to_all(parts, ("cfg", "col"), split_axis=0, concat_axis=0, tiled=True)
    outs = update(timestep, parts, latent.T, vis_hidden.shape[2])
    return tuple(o.T for o in outs)


def solution(mesh):
    req, cfg, sp = mesh.devices.shape
    fine = jax.sharding.Mesh(
        mesh.devices.reshape(req, cfg, 2, sp // 2), ("req", "cfg", "row", "col")
    )
    tokens = ("req", "row", "col")
    out = P(tokens, "cfg")
    return jax.shard_map(
        shards,
        mesh=fine,
        in_specs=(
            P("cfg", tokens, None, None, None),
            P("cfg", tokens, None, None, None),
            P("cfg", "req"),
            P("cfg", tokens, None),
            P(None, ("cfg", "row", "col")),
            P("cfg", "req", None),
            P(),
            out,
            P("req"),
        ),
        out_specs=(out, out, out),
        check_vma=False,
    )
```

```python
import functools
import math

import jax
import jax.numpy as jnp
from jax import lax
from jax.experimental import pallas as pl
from jax.experimental.pallas import tpu as pltpu
from jax.sharding import PartitionSpec as P

STEPS = 64
SMALL = 16 << 20
LARGE = 56 << 20
MOST = 51 << 20
STAGE = 10 << 20
NEG = -1e30
BF = jnp.bfloat16
F32 = jnp.float32
ANY = pl.BlockSpec(memory_space=pltpu.HBM)
WHOLE = pl.BlockSpec(memory_space=pltpu.VMEM)
SCALARS = pl.BlockSpec(memory_space=pltpu.SMEM)
NT = (((1,), (1,)), ((), ()))


def windows(core, row, width):
    starts = []
    for c in (core, 1 - core):
        for r in (row, 1 - row):
            starts.append(pl.ds(pl.multiple_of((2 * c + r) * width, 128), width))
    return starts


def pack_kernel(vis_ref, txt_ref, o_ref, v_ref, t_ref, out_ref, in_sem, out_sem):
    vis, txt = v_ref.shape[1], t_ref.shape[1]
    loads = [
        pltpu.make_async_copy(vis_ref.at[0, :, j], v_ref.at[j], in_sem.at[j]) for j in range(3)
    ] + [
        pltpu.make_async_copy(txt_ref.at[0, :, j], t_ref.at[j], in_sem.at[3 + j]) for j in range(2)
    ]
    for load in loads:
        load.start()
    stores = []
    at = 0
    for j in range(5):
        loads[j].wait()
        block = v_ref[j] if j < 3 else t_ref[j - 3]
        rows = vis if j < 3 else txt
        out_ref[:, at : at + rows, :] = jnp.swapaxes(block, 0, 1)
        stores.append(
            pltpu.make_async_copy(
                out_ref.at[:, at : at + rows, :], o_ref.at[:, at : at + rows, :], out_sem.at[j]
            )
        )
        stores[-1].start()
        at += rows
    for store in stores:
        store.wait()


def pack(vis_qkv, text_kv):
    _, vis, _, heads, width = vis_qkv.shape
    txt = text_kv.shape[1]
    rows = 3 * vis + 2 * txt
    return pl.pallas_call(
        pack_kernel,
        in_specs=[ANY, ANY],
        out_specs=ANY,
        out_shape=jax.ShapeDtypeStruct((heads, rows, width), BF),
        scratch_shapes=[
            pltpu.VMEM((3, vis, heads, width), BF),
            pltpu.VMEM((2, txt, heads, width), BF),
            pltpu.VMEM((heads, rows, width), BF),
            pltpu.SemaphoreType.DMA((5,)),
            pltpu.SemaphoreType.DMA((5,)),
        ],
        compiler_params=pltpu.CompilerParams(vmem_limit_bytes=LARGE),
        cost_estimate=pl.CostEstimate(
            flops=0, bytes_accessed=4 * heads * rows * width, transcendentals=0
        ),
        name="pack",
    )(vis_qkv, text_kv)


def share_kernel(hid_hbm, *refs):
    sends, (hid_ref, sem) = refs[:4], refs[4:]
    load = pltpu.make_async_copy(hid_hbm.at[0], hid_ref, sem)
    load.start()
    core, row, col = (lax.axis_index(a) for a in ("cfg", "row", "col"))
    part = sends[0].shape[1] // 4
    load.wait()
    for me in range(4):

        @pl.when(col == me)
        def _():
            for g, window in enumerate(windows(core, row, 4 * part)):
                hid = hid_ref[:, window]
                for d in range(4):
                    there = me ^ d
                    at = slice(there * part, (there + 1) * part)
                    sends[d][:, g * part : (g + 1) * part] = hid[:, at]


def share(hidden):
    _, vis, width = hidden.shape
    return pl.pallas_call(
        share_kernel,
        in_specs=[ANY],
        out_specs=[WHOLE] * 4,
        out_shape=[jax.ShapeDtypeStruct((vis, width // 4), BF)] * 4,
        scratch_shapes=[pltpu.VMEM((vis, width), BF), pltpu.SemaphoreType.DMA],
        compiler_params=pltpu.CompilerParams(vmem_limit_bytes=53 << 20),
        name="share",
    )(hidden)


def attend_kernel(len_ref, x_ref, o_hbm, k_ref, v_ref, o_ref, sem):
    src, heads, rows, width = x_ref.shape
    cols = src // 2
    vis = o_ref.shape[2] // 2
    txt = (rows - 3 * vis) // 2
    nv = src * vis
    keys = k_ref.shape[1]
    valid = lax.broadcasted_iota(jnp.int32, (1, keys - nv), 1) < len_ref[0]
    scale = math.log2(math.e) / math.sqrt(width)
    ones = jnp.ones((keys, width), BF)
    stores = []
    for h in range(heads):
        for i in range(src):
            at, t0 = slice(i * vis, (i + 1) * vis), nv + i * txt
            k_ref[h, at, :] = x_ref[i, h, vis : 2 * vis, :]
            v_ref[h, at, :width] = x_ref[i, h, 2 * vis : 3 * vis, :]
            k_ref[h, t0 : t0 + txt, :] = x_ref[i, h, 3 * vis : 3 * vis + txt, :]
            v_ref[h, t0 : t0 + txt, :width] = x_ref[i, h, 3 * vis + txt : 3 * vis + 2 * txt, :]
        v_ref[h, :, width:] = ones
        for i in range(0, src, 2):
            q = jnp.concatenate([x_ref[i, h, 0:vis, :], x_ref[i + 1, h, 0:vis, :]], axis=0)
            s = lax.dot_general(q, k_ref[h], NT, preferred_element_type=F32)
            s = jnp.concatenate([s[:, :nv], jnp.where(valid, s[:, nv:], NEG)], axis=1)
            e = jnp.exp2((s - jnp.max(s, axis=1, keepdims=True)) * scale)
            o = jnp.dot(e.astype(BF), v_ref[h], preferred_element_type=F32)
            n = h * src + i
            o_ref[h, i // 2] = (o[:, :width] / o[:, width:]).astype(BF)
            row, at = i // cols, (i % cols) * vis
            for d in range(row * cols, (row + 1) * cols):
                stores.append(
                    pltpu.make_async_copy(
                        o_ref.at[h, i // 2], o_hbm.at[d, h, pl.ds(at, 2 * vis)], sem.at[n + d % 2]
                    )
                )
                stores[-1].start()
    for store in stores:
        store.wait()


def attend(length, x, vis):
    src, heads, rows, width = x.shape
    txt = (rows - 3 * vis) // 2
    keys = src * (vis + txt)
    return pl.pallas_call(
        attend_kernel,
        in_specs=[SCALARS, WHOLE],
        out_specs=ANY,
        out_shape=jax.ShapeDtypeStruct((src, heads, src // 2 * vis, width), BF),
        scratch_shapes=[
            pltpu.VMEM((heads, keys, width), BF),
            pltpu.VMEM((heads, keys, 2 * width), BF),
            pltpu.VMEM((heads, src // 2, 2 * vis, width), BF),
            pltpu.SemaphoreType.DMA((heads * src,)),
        ],
        compiler_params=pltpu.CompilerParams(vmem_limit_bytes=SMALL),
        cost_estimate=pl.CostEstimate(
            flops=4 * heads * src * vis * keys * width,
            bytes_accessed=2 * x.size + 4 * heads * src * vis * width,
            transcendentals=heads * src * vis * keys,
        ),
        name="attend",
    )(length, x)


def split2(x):
    hi = x.astype(BF)
    return hi, (x - hi.astype(F32)).astype(BF)


def split3(x):
    a = x.astype(BF)
    rest = x - a.astype(F32)
    b = rest.astype(BF)
    return a, b, (rest - b.astype(F32)).astype(BF)


def places(cols, vis, patch):
    rows = 2 * patch + 16
    hidden, tables = [], []
    for k in range(4):
        at, across = (k // 2) * vis, (k % 2) * 4 * cols
        hidden.append((slice(at, at + vis), slice(across, across + 4 * cols)))
        at, across = (k // 2) * rows, 8 * cols + (k % 2) * (cols + 64)
        tables.append((slice(at, at + rows), slice(across, across + cols + 64)))
    return hidden, tables


def stage_kernel(mod_hbm, fin_hbm, *refs):
    w_hbm, got_hbm, (aux_ref, out_hbm) = refs[:4], refs[4:8], refs[8:10]
    mod_ref, fin_ref, w_ref, sem = refs[10:]
    core, row, col = (lax.axis_index(a) for a in ("cfg", "row", "col"))
    part, vis = w_hbm[0].shape[0], got_hbm[0].shape[0]
    patch = fin_ref.shape[0]
    hidden, tables = places(part, vis, patch)
    loads = [
        pltpu.make_async_copy(mod_hbm.at[0], mod_ref, sem.at[0]),
        pltpu.make_async_copy(fin_hbm, fin_ref, sem.at[1]),
    ]
    moves = [
        pltpu.make_async_copy(w_hbm[g], w_ref.at[g * part : (g + 1) * part], sem.at[2 + g])
        for g in range(4)
    ]
    for load in loads + moves:
        load.start()
    for load in loads:
        load.wait()
    for me in range(4):

        @pl.when(col == me)
        def _():
            copies = [
                pltpu.make_async_copy(got_hbm[d], aux_ref.at[hidden[me ^ d]], sem.at[6 + d])
                for d in range(4)
            ]
            for copy in copies:
                copy.start()
            own = slice(me * part, (me + 1) * part)
            total, shift = 0.0, 0.0
            for g, window in enumerate(windows(core, row, 4 * part)):
                f = fin_ref[:, window].astype(F32)[:, own]
                scaled = f * (1.0 + mod_ref[1:2, window][:, own])
                total = total + jnp.sum(scaled, axis=1, keepdims=True)
                moved = f * mod_ref[2:3, window][:, own]
                shift = shift + jnp.sum(moved, axis=1, keepdims=True)
                hi, lo = split2(scaled)
                gate = split3(jnp.broadcast_to(mod_ref[0:1, window][:, own], (16, part)))
                line = lax.broadcasted_iota(jnp.int32, (16, part), 0)
                gate = jnp.where(line == 0, gate[0], jnp.where(line == 1, gate[1], gate[2]))
                both = jnp.concatenate([hi, lo, gate], axis=0)
                extra = jnp.zeros((both.shape[0], 64), BF)
                if g == 3:
                    lane = lax.broadcasted_iota(jnp.int32, (patch, 64), 1)
                    pieces = split3(jnp.where(lane % 2 == 0, total, shift))
                    pieces = jnp.where(
                        lane < 2, pieces[0], jnp.where(lane < 4, pieces[1], pieces[2])
                    )
                    extra = jnp.concatenate([pieces, extra[patch:]], axis=0)
                aux_ref[tables[g]] = jnp.concatenate([both, extra], axis=1)
            for copy in copies:
                copy.wait()

    for move in moves:
        move.wait()
    store = pltpu.make_async_copy(w_ref, out_hbm, sem.at[0])
    store.start()
    store.wait()


def stage(modulation, final_t, blocks, got):
    patch, width = final_t.shape
    cols, depth = blocks[0].shape
    rows = 2 * max(got[0].shape[0], 2 * patch + 16)
    return pl.pallas_call(
        stage_kernel,
        in_specs=[ANY] * 10,
        out_specs=[WHOLE, ANY],
        out_shape=[
            jax.ShapeDtypeStruct((rows, depth), BF),
            jax.ShapeDtypeStruct((4 * cols, depth), BF),
        ],
        scratch_shapes=[
            pltpu.VMEM(modulation.shape[1:], F32),
            pltpu.VMEM(final_t.shape, BF),
            pltpu.VMEM((4 * cols, depth), BF),
            pltpu.SemaphoreType.DMA((10,)),
        ],
        compiler_params=pltpu.CompilerParams(vmem_limit_bytes=48 << 20),
        cost_estimate=pl.CostEstimate(flops=2 * 10**10, bytes_accessed=0, transcendentals=0),
        name="stage",
    )(modulation, final_t, *blocks, *got)


def project_kernel(a_ref, aux_ref, w_hbm, o_ref, w_ref, r_ref, sem):
    chunks, tokens, depth = a_ref.shape
    part = r_ref.shape[2]
    vis, patch = tokens // 4, 2 * o_ref.shape[1] - 16
    hidden, tables = places(part, vis, patch)
    loads = []
    for g in range(4):
        at = slice(g * part, (g + 1) * part)
        loads.append(pltpu.make_async_copy(w_hbm.at[at], w_ref.at[at], sem.at[g]))
        loads[g].start()
    for g in range(4):
        for k, (rows, c) in enumerate(hidden):
            h = aux_ref[rows, c.start + g * part : c.start + (g + 1) * part]
            r_ref[g, k * vis : (k + 1) * vis, :] = h.astype(F32)
    lhs = jnp.concatenate([a_ref[i] for i in range(chunks)], axis=1)
    total = 0.0
    for g in range(4):
        if g % 2 == 0:
            loads[g].wait()
            loads[g + 1].wait()
        w = w_ref[g * part : (g + 1) * part, :]
        p = lax.dot_general(lhs, w, NT, preferred_element_type=F32)
        rows, c = tables[g]
        gate = aux_ref[rows.start + 2 * patch : rows.stop, c.start : c.start + part].astype(F32)
        r = r_ref[g] + (gate[0:1] + gate[1:2] + gate[2:3]) * p
        r_ref[g] = r
        total = total + r
    mean = jnp.sum(total, axis=1, keepdims=True) * (1.0 / (4 * part))
    spread, both, fine = 0.0, 0.0, 0.0
    for g in range(4):
        d = r_ref[g] - mean
        spread = spread + d * d
        hi, lo = split2(d)
        rows, c = tables[g]
        w = aux_ref[rows.start : rows.start + 2 * patch, c.start : c.start + part]
        both = both + lax.dot_general(hi, w, NT, preferred_element_type=F32)
        fine = fine + lax.dot_general(lo, w[:patch], NT, preferred_element_type=F32)
    pred = both[:, :patch] + both[:, patch:] + fine
    stats = [mean, jnp.sum(spread, axis=1, keepdims=True), jnp.zeros((tokens, 78), F32)]
    pred = jnp.transpose(jnp.concatenate([pred, *stats], axis=1))
    rows, c = tables[3]
    sums = aux_ref[rows.start : rows.start + patch, c.start + part : c.stop].astype(F32)
    sums = (sums[:, :32] + sums[:, 2:34]) + sums[:, 4:36]
    half = patch // 2
    for core in range(2):
        for k in range(4):
            at = slice(k * vis, (k + 1) * vis)
            rows = slice(core * half, (core + 1) * half)
            o_ref[core * 4 + k, :half] = jnp.concatenate([pred[rows, at], sums[rows]], axis=1)
            o_ref[core * 4 + k, half:] = jnp.concatenate(
                [pred[patch : patch + 8, at], sums[:8]], axis=1
            )


def project(att, aux, weights, patch):
    chunks, tokens, width = att.shape
    depth = chunks * width
    cols = weights.shape[0] // 4
    return pl.pallas_call(
        project_kernel,
        in_specs=[WHOLE, WHOLE, ANY],
        out_specs=WHOLE,
        out_shape=jax.ShapeDtypeStruct((8, patch // 2 + 8, 128), F32),
        scratch_shapes=[
            pltpu.VMEM(weights.shape, BF),
            pltpu.VMEM((4, tokens, cols), F32),
            pltpu.SemaphoreType.DMA((4,)),
        ],
        compiler_params=pltpu.CompilerParams(vmem_limit_bytes=MOST),
        cost_estimate=pl.CostEstimate(
            flops=8 * cols * depth * tokens,
            bytes_accessed=8 * cols * depth,
            transcendentals=0,
        ),
        name="project",
    )(att, aux, weights)


def update_kernel(step_ref, x_ref, lat_ref, vel_ref, next_ref, den_ref, *, count):
    half, vis = lat_ref.shape
    preds = []
    for b in range(2):
        parts = [x_ref[b * 4 + k] for k in range(4)]
        means = [t[half : half + 1, :vis] for t in parts]
        mean = 0.25 * (means[0] + means[1] + means[2] + means[3])
        spread, linear, shift = 0.0, 0.0, 0.0
        for k in range(4):
            off = means[k] - mean
            spread = spread + parts[k][half + 1 : half + 2, :vis] + (0.25 * count) * (off * off)
            linear = linear + parts[k][:half, :vis] + parts[k][:half, vis : vis + 1] * off
            shift = shift + parts[k][:half, vis + 1 : vis + 2]
        preds.append(linear * lax.rsqrt(spread * (1.0 / count) + 1e-06) + shift)
    cond, uncond = preds
    velocity = uncond + 4.5 * (cond - uncond)
    step_now = step_ref[0].astype(F32)
    remain_now = 1.0 - step_now * (1.0 / STEPS)
    remain_next = 1.0 - (step_now + 1.0) * (1.0 / STEPS)
    sigma_now = remain_now * remain_now
    sigma_next = remain_next * remain_next
    latent = lat_ref[...]
    vel_ref[...] = velocity
    next_ref[...] = latent + (sigma_next - sigma_now) * velocity
    den_ref[...] = latent - sigma_now * velocity


def update(timestep, parts, latent, count):
    return pl.pallas_call(
        functools.partial(update_kernel, count=count),
        in_specs=[SCALARS, WHOLE, WHOLE],
        out_specs=[WHOLE] * 3,
        out_shape=[jax.ShapeDtypeStruct(latent.shape, F32)] * 3,
        compiler_params=pltpu.CompilerParams(vmem_limit_bytes=2 << 20),
        name="update",
    )(timestep, parts, latent)


def across_outer(reqs):
    deep = 8
    if reqs % deep:
        return None
    high = reqs // deep
    pairs = []
    for r in range(reqs):
        for s in range(8):
            y = 2 * (r // deep) + s // 4
            near = (y + 1 if y % 2 else y - 1) % (2 * high)
            pairs.append((r * 8 + s, (near // 2 * deep + r % deep) * 8 + near % 2 * 4 + s % 4))
    return pairs


def shards(
    vis_qkv, text_kv, text_len, vis_hidden, out_weight, modulation, final_weight, latent, timestep
):
    vis, txt = vis_qkv.shape[1], text_kv.shape[1]
    cores = [(0, 1), (1, 0)]
    outer = across_outer(lax.axis_size("req"))

    own = out_weight.T

    def across(block):
        if outer is None:
            return lax.ppermute(block, "row", cores)
        return lax.ppermute(block, ("req", "row", "col"), outer)

    far = across(own)
    packed, hidden = lax.optimization_barrier((pack(vis_qkv, text_kv), vis_hidden))
    mine, *sends = share(hidden)
    heads = lax.all_to_all(
        packed, ("row", "col"), split_axis=0, concat_axis=0, tiled=True
    ).reshape(8, 2, 3 * vis + 2 * txt, 128)
    got = [mine] + [
        lax.ppermute(block, "col", [(c, c ^ d) for c in range(4)])
        for d, block in zip((1, 2, 3), sends)
    ]
    attended = attend(text_len[0], heads, vis)
    far, modulation, *got = lax.optimization_barrier((far, modulation, *got))
    own_other, far_other = (lax.ppermute(b, "cfg", cores) for b in (own, far))
    aux, weights = stage(modulation, final_weight.T, [own, far, own_other, far_other], got)
    att = lax.all_to_all(
        attended, ("row", "col"), split_axis=0, concat_axis=0, tiled=True
    ).reshape(16, 4 * vis, 128)
    parts = project(att, aux, weights, final_weight.shape[1])
    parts = lax.all_to_all(parts, ("cfg", "col"), split_axis=0, concat_axis=0, tiled=True)
    outs = update(timestep, parts, latent.T, vis_hidden.shape[2])
    return tuple(o.T for o in outs)


def solution(mesh):
    req, cfg, sp = mesh.devices.shape
    fine = jax.sharding.Mesh(
        mesh.devices.reshape(req, cfg, 2, sp // 2), ("req", "cfg", "row", "col")
    )
    tokens = ("req", "row", "col")
    out = P(tokens, "cfg")
    return jax.shard_map(
        shards,
        mesh=fine,
        in_specs=(
            P("cfg", tokens, None, None, None),
            P("cfg", tokens, None, None, None),
            P("cfg", "req"),
            P("cfg", tokens, None),
            P(None, ("cfg", "row", "col")),
            P("cfg", "req", None),
            P(),
            out,
            P("req"),
        ),
        out_specs=(out, out, out),
        check_vma=False,
    )
```

```python
import functools
import math

import jax
import jax.numpy as jnp
from jax import lax
from jax.experimental import pallas as pl
from jax.experimental.pallas import tpu as pltpu
from jax.sharding import PartitionSpec as P

STEPS = 64
SMALL = 16 << 20
LARGE = 56 << 20
MOST = 51 << 20
STAGE = 10 << 20
NEG = -1e30
BF = jnp.bfloat16
F32 = jnp.float32
ANY = pl.BlockSpec(memory_space=pltpu.HBM)
WHOLE = pl.BlockSpec(memory_space=pltpu.VMEM)
SCALARS = pl.BlockSpec(memory_space=pltpu.SMEM)
NT = (((1,), (1,)), ((), ()))


def windows(core, row, width):
    starts = []
    for c in (core, 1 - core):
        for r in (row, 1 - row):
            starts.append(pl.ds(pl.multiple_of((2 * c + r) * width, 128), width))
    return starts


def pack_kernel(vis_ref, txt_ref, o_ref, v_ref, t_ref, out_ref, in_sem, out_sem):
    vis, txt = v_ref.shape[1], t_ref.shape[1]
    loads = [
        pltpu.make_async_copy(vis_ref.at[0, :, j], v_ref.at[j], in_sem.at[j]) for j in range(3)
    ] + [
        pltpu.make_async_copy(txt_ref.at[0, :, j], t_ref.at[j], in_sem.at[3 + j]) for j in range(2)
    ]
    for load in loads:
        load.start()
    stores = []
    at = 0
    for j in range(5):
        loads[j].wait()
        block = v_ref[j] if j < 3 else t_ref[j - 3]
        rows = vis if j < 3 else txt
        out_ref[:, at : at + rows, :] = jnp.swapaxes(block, 0, 1)
        stores.append(
            pltpu.make_async_copy(
                out_ref.at[:, at : at + rows, :], o_ref.at[:, at : at + rows, :], out_sem.at[j]
            )
        )
        stores[-1].start()
        at += rows
    for store in stores:
        store.wait()


def pack(vis_qkv, text_kv):
    _, vis, _, heads, width = vis_qkv.shape
    txt = text_kv.shape[1]
    rows = 3 * vis + 2 * txt
    return pl.pallas_call(
        pack_kernel,
        in_specs=[ANY, ANY],
        out_specs=ANY,
        out_shape=jax.ShapeDtypeStruct((heads, rows, width), BF),
        scratch_shapes=[
            pltpu.VMEM((3, vis, heads, width), BF),
            pltpu.VMEM((2, txt, heads, width), BF),
            pltpu.VMEM((heads, rows, width), BF),
            pltpu.SemaphoreType.DMA((5,)),
            pltpu.SemaphoreType.DMA((5,)),
        ],
        compiler_params=pltpu.CompilerParams(vmem_limit_bytes=LARGE),
        cost_estimate=pl.CostEstimate(
            flops=0, bytes_accessed=4 * heads * rows * width, transcendentals=0
        ),
        name="pack",
    )(vis_qkv, text_kv)


def share_kernel(hid_hbm, *refs):
    sends, (hid_ref, sem) = refs[:4], refs[4:]
    load = pltpu.make_async_copy(hid_hbm.at[0], hid_ref, sem)
    load.start()
    core, row, col = (lax.axis_index(a) for a in ("cfg", "row", "col"))
    part = sends[0].shape[1] // 4
    load.wait()
    for me in range(4):

        @pl.when(col == me)
        def _():
            for g, window in enumerate(windows(core, row, 4 * part)):
                hid = hid_ref[:, window]
                for d in range(4):
                    there = me ^ d
                    at = slice(there * part, (there + 1) * part)
                    sends[d][:, g * part : (g + 1) * part] = hid[:, at]


def share(hidden):
    _, vis, width = hidden.shape
    return pl.pallas_call(
        share_kernel,
        in_specs=[ANY],
        out_specs=[WHOLE] * 4,
        out_shape=[jax.ShapeDtypeStruct((vis, width // 4), BF)] * 4,
        scratch_shapes=[pltpu.VMEM((vis, width), BF), pltpu.SemaphoreType.DMA],
        compiler_params=pltpu.CompilerParams(vmem_limit_bytes=LARGE),
        name="share",
    )(hidden)


def attend_kernel(len_ref, x_ref, o_hbm, k_ref, v_ref, o_ref, sem):
    src, heads, rows, width = x_ref.shape
    cols = src // 2
    vis = o_ref.shape[2] // 2
    txt = (rows - 3 * vis) // 2
    nv = src * vis
    keys = k_ref.shape[1]
    valid = lax.broadcasted_iota(jnp.int32, (1, keys - nv), 1) < len_ref[0]
    scale = math.log2(math.e) / math.sqrt(width)
    ones = jnp.ones((keys, width), BF)
    stores = []
    for h in range(heads):
        for i in range(src):
            at, t0 = slice(i * vis, (i + 1) * vis), nv + i * txt
            k_ref[h, at, :] = x_ref[i, h, vis : 2 * vis, :]
            v_ref[h, at, :width] = x_ref[i, h, 2 * vis : 3 * vis, :]
            k_ref[h, t0 : t0 + txt, :] = x_ref[i, h, 3 * vis : 3 * vis + txt, :]
            v_ref[h, t0 : t0 + txt, :width] = x_ref[i, h, 3 * vis + txt : 3 * vis + 2 * txt, :]
        v_ref[h, :, width:] = ones
        for i in range(0, src, 2):
            q = jnp.concatenate([x_ref[i, h, 0:vis, :], x_ref[i + 1, h, 0:vis, :]], axis=0)
            s = lax.dot_general(q, k_ref[h], NT, preferred_element_type=F32)
            s = jnp.concatenate([s[:, :nv], jnp.where(valid, s[:, nv:], NEG)], axis=1)
            e = jnp.exp2((s - jnp.max(s, axis=1, keepdims=True)) * scale)
            o = jnp.dot(e.astype(BF), v_ref[h], preferred_element_type=F32)
            n = h * src + i
            o_ref[h, i // 2] = (o[:, :width] / o[:, width:]).astype(BF)
            row, at = i // cols, (i % cols) * vis
            for d in range(row * cols, (row + 1) * cols):
                stores.append(
                    pltpu.make_async_copy(
                        o_ref.at[h, i // 2], o_hbm.at[d, h, pl.ds(at, 2 * vis)], sem.at[n + d % 2]
                    )
                )
                stores[-1].start()
    for store in stores:
        store.wait()


def attend(length, x, vis):
    src, heads, rows, width = x.shape
    txt = (rows - 3 * vis) // 2
    keys = src * (vis + txt)
    return pl.pallas_call(
        attend_kernel,
        in_specs=[SCALARS, WHOLE],
        out_specs=ANY,
        out_shape=jax.ShapeDtypeStruct((src, heads, src // 2 * vis, width), BF),
        scratch_shapes=[
            pltpu.VMEM((heads, keys, width), BF),
            pltpu.VMEM((heads, keys, 2 * width), BF),
            pltpu.VMEM((heads, src // 2, 2 * vis, width), BF),
            pltpu.SemaphoreType.DMA((heads * src,)),
        ],
        compiler_params=pltpu.CompilerParams(vmem_limit_bytes=SMALL),
        cost_estimate=pl.CostEstimate(
            flops=4 * heads * src * vis * keys * width,
            bytes_accessed=2 * x.size + 4 * heads * src * vis * width,
            transcendentals=heads * src * vis * keys,
        ),
        name="attend",
    )(length, x)


def split2(x):
    hi = x.astype(BF)
    return hi, (x - hi.astype(F32)).astype(BF)


def split3(x):
    a = x.astype(BF)
    rest = x - a.astype(F32)
    b = rest.astype(BF)
    return a, b, (rest - b.astype(F32)).astype(BF)


def places(cols, vis, patch):
    rows = 2 * patch + 16
    hidden, tables = [], []
    for k in range(4):
        at, across = (k // 2) * vis, (k % 2) * 4 * cols
        hidden.append((slice(at, at + vis), slice(across, across + 4 * cols)))
        at, across = (k // 2) * rows, 8 * cols + (k % 2) * (cols + 64)
        tables.append((slice(at, at + rows), slice(across, across + cols + 64)))
    return hidden, tables


def stage_kernel(mod_hbm, fin_hbm, *refs):
    w_hbm, got_hbm, (aux_ref, out_hbm) = refs[:4], refs[4:8], refs[8:10]
    mod_ref, fin_ref, w_ref, sem = refs[10:]
    core, row, col = (lax.axis_index(a) for a in ("cfg", "row", "col"))
    part, vis = w_hbm[0].shape[0], got_hbm[0].shape[0]
    patch = fin_ref.shape[0]
    hidden, tables = places(part, vis, patch)
    loads = [
        pltpu.make_async_copy(mod_hbm.at[0], mod_ref, sem.at[0]),
        pltpu.make_async_copy(fin_hbm, fin_ref, sem.at[1]),
    ]
    moves = [
        pltpu.make_async_copy(w_hbm[g], w_ref.at[g * part : (g + 1) * part], sem.at[2 + g])
        for g in range(4)
    ]
    for load in loads + moves:
        load.start()
    for load in loads:
        load.wait()
    for me in range(4):

        @pl.when(col == me)
        def _():
            copies = [
                pltpu.make_async_copy(got_hbm[d], aux_ref.at[hidden[me ^ d]], sem.at[6 + d])
                for d in range(4)
            ]
            for copy in copies:
                copy.start()
            own = slice(me * part, (me + 1) * part)
            total, shift = 0.0, 0.0
            for g, window in enumerate(windows(core, row, 4 * part)):
                f = fin_ref[:, window].astype(F32)[:, own]
                scaled = f * (1.0 + mod_ref[1:2, window][:, own])
                total = total + jnp.sum(scaled, axis=1, keepdims=True)
                moved = f * mod_ref[2:3, window][:, own]
                shift = shift + jnp.sum(moved, axis=1, keepdims=True)
                hi, lo = split2(scaled)
                gate = split3(jnp.broadcast_to(mod_ref[0:1, window][:, own], (16, part)))
                line = lax.broadcasted_iota(jnp.int32, (16, part), 0)
                gate = jnp.where(line == 0, gate[0], jnp.where(line == 1, gate[1], gate[2]))
                both = jnp.concatenate([hi, lo, gate], axis=0)
                extra = jnp.zeros((both.shape[0], 64), BF)
                if g == 3:
                    lane = lax.broadcasted_iota(jnp.int32, (patch, 64), 1)
                    pieces = split3(jnp.where(lane % 2 == 0, total, shift))
                    pieces = jnp.where(
                        lane < 2, pieces[0], jnp.where(lane < 4, pieces[1], pieces[2])
                    )
                    extra = jnp.concatenate([pieces, extra[patch:]], axis=0)
                aux_ref[tables[g]] = jnp.concatenate([both, extra], axis=1)
            for copy in copies:
                copy.wait()

    for move in moves:
        move.wait()
    store = pltpu.make_async_copy(w_ref, out_hbm, sem.at[0])
    store.start()
    store.wait()


def stage(modulation, final_t, blocks, got):
    patch, width = final_t.shape
    cols, depth = blocks[0].shape
    rows = 2 * max(got[0].shape[0], 2 * patch + 16)
    return pl.pallas_call(
        stage_kernel,
        in_specs=[ANY] * 10,
        out_specs=[WHOLE, ANY],
        out_shape=[
            jax.ShapeDtypeStruct((rows, depth), BF),
            jax.ShapeDtypeStruct((4 * cols, depth), BF),
        ],
        scratch_shapes=[
            pltpu.VMEM(modulation.shape[1:], F32),
            pltpu.VMEM(final_t.shape, BF),
            pltpu.VMEM((4 * cols, depth), BF),
            pltpu.SemaphoreType.DMA((10,)),
        ],
        compiler_params=pltpu.CompilerParams(vmem_limit_bytes=STAGE),
        cost_estimate=pl.CostEstimate(flops=2 * 10**10, bytes_accessed=0, transcendentals=0),
        name="stage",
    )(modulation, final_t, *blocks, *got)


def project_kernel(a_ref, aux_ref, w_hbm, o_ref, w_ref, r_ref, sem):
    chunks, tokens, depth = a_ref.shape
    part = r_ref.shape[2]
    vis, patch = tokens // 4, 2 * o_ref.shape[1] - 16
    hidden, tables = places(part, vis, patch)
    loads = []
    for g in range(4):
        at = slice(g * part, (g + 1) * part)
        loads.append(pltpu.make_async_copy(w_hbm.at[at], w_ref.at[at], sem.at[g]))
        loads[g].start()
    for g in range(4):
        for k, (rows, c) in enumerate(hidden):
            h = aux_ref[rows, c.start + g * part : c.start + (g + 1) * part]
            r_ref[g, k * vis : (k + 1) * vis, :] = h.astype(F32)
    lhs = jnp.concatenate([a_ref[i] for i in range(chunks)], axis=1)
    total = 0.0
    for g in range(4):
        if g % 2 == 0:
            loads[g].wait()
            loads[g + 1].wait()
        w = w_ref[g * part : (g + 1) * part, :]
        p = lax.dot_general(lhs, w, NT, preferred_element_type=F32)
        rows, c = tables[g]
        gate = aux_ref[rows.start + 2 * patch : rows.stop, c.start : c.start + part].astype(F32)
        r = r_ref[g] + (gate[0:1] + gate[1:2] + gate[2:3]) * p
        r_ref[g] = r
        total = total + r
    mean = jnp.sum(total, axis=1, keepdims=True) * (1.0 / (4 * part))
    spread, both, fine = 0.0, 0.0, 0.0
    for g in range(4):
        d = r_ref[g] - mean
        spread = spread + d * d
        hi, lo = split2(d)
        rows, c = tables[g]
        w = aux_ref[rows.start : rows.start + 2 * patch, c.start : c.start + part]
        both = both + lax.dot_general(hi, w, NT, preferred_element_type=F32)
        fine = fine + lax.dot_general(lo, w[:patch], NT, preferred_element_type=F32)
    pred = both[:, :patch] + both[:, patch:] + fine
    stats = [mean, jnp.sum(spread, axis=1, keepdims=True), jnp.zeros((tokens, 78), F32)]
    pred = jnp.transpose(jnp.concatenate([pred, *stats], axis=1))
    rows, c = tables[3]
    sums = aux_ref[rows.start : rows.start + patch, c.start + part : c.stop].astype(F32)
    sums = (sums[:, :32] + sums[:, 2:34]) + sums[:, 4:36]
    half = patch // 2
    for core in range(2):
        for k in range(4):
            at = slice(k * vis, (k + 1) * vis)
            rows = slice(core * half, (core + 1) * half)
            o_ref[k * 2 + core, :half] = jnp.concatenate([pred[rows, at], sums[rows]], axis=1)
            o_ref[k * 2 + core, half:] = jnp.concatenate(
                [pred[patch : patch + 8, at], sums[:8]], axis=1
            )


def project(att, aux, weights, patch):
    chunks, tokens, width = att.shape
    depth = chunks * width
    cols = weights.shape[0] // 4
    return pl.pallas_call(
        project_kernel,
        in_specs=[WHOLE, WHOLE, ANY],
        out_specs=WHOLE,
        out_shape=jax.ShapeDtypeStruct((8, patch // 2 + 8, 128), F32),
        scratch_shapes=[
            pltpu.VMEM(weights.shape, BF),
            pltpu.VMEM((4, tokens, cols), F32),
            pltpu.SemaphoreType.DMA((4,)),
        ],
        compiler_params=pltpu.CompilerParams(vmem_limit_bytes=MOST),
        cost_estimate=pl.CostEstimate(
            flops=8 * cols * depth * tokens,
            bytes_accessed=8 * cols * depth,
            transcendentals=0,
        ),
        name="project",
    )(att, aux, weights)


def update_kernel(step_ref, x_ref, lat_ref, vel_ref, next_ref, den_ref, *, count):
    half, vis = lat_ref.shape
    preds = []
    for b in range(2):
        parts = [x_ref[k * 2 + b] for k in range(4)]
        means = [t[half : half + 1, :vis] for t in parts]
        mean = 0.25 * (means[0] + means[1] + means[2] + means[3])
        spread, linear, shift = 0.0, 0.0, 0.0
        for k in range(4):
            off = means[k] - mean
            spread = spread + parts[k][half + 1 : half + 2, :vis] + (0.25 * count) * (off * off)
            linear = linear + parts[k][:half, :vis] + parts[k][:half, vis : vis + 1] * off
            shift = shift + parts[k][:half, vis + 1 : vis + 2]
        preds.append(linear * lax.rsqrt(spread * (1.0 / count) + 1e-06) + shift)
    cond, uncond = preds
    velocity = uncond + 4.5 * (cond - uncond)
    step_now = step_ref[0].astype(F32)
    remain_now = 1.0 - step_now * (1.0 / STEPS)
    remain_next = 1.0 - (step_now + 1.0) * (1.0 / STEPS)
    sigma_now = remain_now * remain_now
    sigma_next = remain_next * remain_next
    latent = lat_ref[...]
    vel_ref[...] = velocity
    next_ref[...] = latent + (sigma_next - sigma_now) * velocity
    den_ref[...] = latent - sigma_now * velocity


def update(timestep, parts, latent, count):
    return pl.pallas_call(
        functools.partial(update_kernel, count=count),
        in_specs=[SCALARS, WHOLE, WHOLE],
        out_specs=[WHOLE] * 3,
        out_shape=[jax.ShapeDtypeStruct(latent.shape, F32)] * 3,
        compiler_params=pltpu.CompilerParams(vmem_limit_bytes=2 << 20),
        name="update",
    )(timestep, parts, latent)


def across_outer(reqs):
    deep = 8
    if reqs % deep:
        return None
    high = reqs // deep
    pairs = []
    for r in range(reqs):
        for s in range(8):
            y = 2 * (r // deep) + s // 4
            near = (y + 1 if y % 2 else y - 1) % (2 * high)
            pairs.append((r * 8 + s, (near // 2 * deep + r % deep) * 8 + near % 2 * 4 + s % 4))
    return pairs


def shards(
    vis_qkv, text_kv, text_len, vis_hidden, out_weight, modulation, final_weight, latent, timestep
):
    vis, txt = vis_qkv.shape[1], text_kv.shape[1]
    cores = [(0, 1), (1, 0)]
    outer = across_outer(lax.axis_size("req"))

    own = out_weight.T

    def across(block):
        if outer is None:
            return lax.ppermute(block, "row", cores)
        return lax.ppermute(block, ("req", "row", "col"), outer)

    far = across(own)
    packed, hidden = lax.optimization_barrier((pack(vis_qkv, text_kv), vis_hidden))
    mine, *sends = share(hidden)
    heads = lax.all_to_all(
        packed, ("row", "col"), split_axis=0, concat_axis=0, tiled=True
    ).reshape(8, 2, 3 * vis + 2 * txt, 128)
    got = [mine] + [
        lax.ppermute(block, "col", [(c, c ^ d) for c in range(4)])
        for d, block in zip((1, 2, 3), sends)
    ]
    attended = attend(text_len[0], heads, vis)
    far, modulation, *got = lax.optimization_barrier((far, modulation, *got))
    own_other, far_other = (lax.ppermute(b, "cfg", cores) for b in (own, far))
    aux, weights = stage(modulation, final_weight.T, [own, far, own_other, far_other], got)
    att = lax.all_to_all(
        attended, ("row", "col"), split_axis=0, concat_axis=0, tiled=True
    ).reshape(16, 4 * vis, 128)
    parts = project(att, aux, weights, final_weight.shape[1])
    parts = lax.all_to_all(parts, ("col", "cfg"), split_axis=0, concat_axis=0, tiled=True)
    outs = update(timestep, parts, latent.T, vis_hidden.shape[2])
    return tuple(o.T for o in outs)


def solution(mesh):
    req, cfg, sp = mesh.devices.shape
    fine = jax.sharding.Mesh(
        mesh.devices.reshape(req, cfg, 2, sp // 2), ("req", "cfg", "row", "col")
    )
    tokens = ("req", "row", "col")
    out = P(tokens, "cfg")
    return jax.shard_map(
        shards,
        mesh=fine,
        in_specs=(
            P("cfg", tokens, None, None, None),
            P("cfg", tokens, None, None, None),
            P("cfg", "req"),
            P("cfg", tokens, None),
            P(None, ("cfg", "row", "col")),
            P("cfg", "req", None),
            P(),
            out,
            P("req"),
        ),
        out_specs=(out, out, out),
        check_vma=False,
    )
```
